32 devices in a mesh: dp: 4 (over x, core), fsdp: 8 (over z, y).
Axes of the slice: x: 2, y: 2, z: 4, core: 2. Of those that a mesh axis runs over, the one named last changes fastest.
Arguments:
- features: bfloat16 [24576, 512], P(('dp', 'fsdp')), may hold values from -8 to 8
- row_valid: int32 [24576], P(('dp', 'fsdp')), may hold values 0 or 1
- micro_batch: int32 [24576], P(('dp', 'fsdp')), may hold values from 0 to 3
- gains: float32 [2, 512], replicated, may hold values from 0.25 to 1.75
- shifts: float32 [2, 512], replicated, may hold values from -4 to 4
- mask_logits: float32 [2, 6, 512], replicated, may hold values from -6 to 6
- thresholds: float32 [2, 6], replicated, may hold values from 0.5 to 2.5
- gate_in: bfloat16 [2, 6, 1024, 1024], P(None, None, 'fsdp'), may hold values from -0.1875 to 0.1875
- bias_in: float32 [2, 6, 1024], replicated, may hold values from -4 to 4
- gate_out: bfloat16 [2, 6, 1024, 512], P(None, None, 'fsdp'), may hold values from -0.1875 to 0.1875
- bias_out: float32 [2, 6, 512], replicated, may hold values from -4 to 4
- cotangent: bfloat16 [24576, 512], P(('dp', 'fsdp')), may hold values from -6 to 6
Outputs:
- mixed_out: bfloat16 [24576, 512], P(('dp', 'fsdp'))
- grad_features: float32 [24576, 512], P(('dp', 'fsdp'))
- grad_gains: float32 [2, 512], replicated
- grad_shifts: float32 [2, 512], replicated
- grad_logits: float32 [2, 6, 512], replicated
- grad_thresholds: float32 [2, 6], replicated
- grad_gate_in: float32 [2, 6, 1024, 1024], P(None, None, 'fsdp')
- grad_bias_in: float32 [2, 6, 1024], replicated
- grad_gate_out: float32 [2, 6, 1024, 512], P(None, None, 'fsdp')
- grad_bias_out: float32 [2, 6, 512], replicated
The draws below stay inside these ranges and needn't reach their ends.
Inputs may be any that keep to these rules, and one draw needn't show every extreme that they name: `row_valid`: 1 marks a real row, 0 a padded one.
All inputs are finite; a program needn't handle non-finite values. No bound on the sum of `row_valid` on one device may be relied on, other than what follows from the above.
Results may differ from the reference program's by a relative error of at most 0.015.
Values may be sent and summed in bfloat16 or wider, within the bound.
No kernel may reach another device: no remote copies, remote signals or barrier semaphores. Data moves between devices by JAX's collectives and lax.ppermute only.
A program may use at most 320 MiB of HBM per device.

```python
import functools
import jax
import jax.numpy as jnp
from jax import lax

F = 512
SECTIONS = 6
LAYERS = 2
MB = 4
ROWS = 24576


def draw_features(key, part):
    key = jax.random.fold_in(key, 11)
    key_rows, key_cols, key_mean = jax.random.split(key, 3)
    position = jnp.arange(ROWS, dtype=jnp.float32)[:, None] / ROWS
    column_scale = jnp.exp(jax.random.uniform(key_cols, (1, F), minval=-0.5, maxval=0.5))
    offsets = 0.5 * jax.random.normal(key_mean, (1, F))
    noise_part = jax.random.normal(key_rows, (ROWS, F))
    values = (0.5 + position) * column_scale * noise_part + offsets
    return jnp.clip(values, -8.0, 8.0).astype(jnp.bfloat16)


def set_ends(array, rng, smallest, high):
    dims = array.shape
    place = [jax.random.randint(jax.random.fold_in(rng, axis), (), 0, dims[axis]) for axis in range(len(dims))]
    array = array.at[tuple(place)].set(smallest)
    longest = dims.index(max(dims))
    place[longest] = (place[longest] + 1) % dims[longest]
    return array.at[tuple(place)].set(high)


def shard_levels(own_key, dims, pieces, least, largest):
    level = 1.0
    for axis_at, shards_of in pieces:
        steps = jax.random.uniform(jax.random.fold_in(jax.random.fold_in(own_key, 6), axis_at), (shards_of,), jnp.float32, least / len(pieces), largest / len(pieces))
        level = level * jnp.repeat(jnp.exp(steps), dims[axis_at] // shards_of).reshape((-1,) + (1,) * (len(dims) - 1 - axis_at))
    return level


def bell_draw(rng, shape, scale, limit, cuts=(), held_as=jnp.bfloat16):
    array = jax.random.normal(rng, shape, jnp.float32) * scale
    if len(cuts) > 0:
        array = shard_levels(rng, shape, cuts, -0.22, 0.18) * array
    return jnp.clip(array, min=-limit, max=limit).astype(held_as)


def setup_inputs(seed: int = 0) -> dict:
    splits = jax.random.split(jax.random.key(seed), 13)
    return {
        "features": draw_features(jax.random.fold_in(splits[12], 71), 0),
        "row_valid": set_ends((jax.random.randint(splits[1], (ROWS,), 0, 4) < 3).astype(jnp.int32), jax.random.fold_in(splits[1], 1), 0, 1),
        "micro_batch": set_ends(jax.random.randint(splits[2], (ROWS,), 0, MB), jax.random.fold_in(splits[2], 1), 0, MB - 1).astype(jnp.int32),
        "gains": jnp.clip(1.0 + 0.15 * jax.random.normal(splits[3], (LAYERS, F), jnp.float32), 0.25, 1.75),
        "shifts": bell_draw(splits[4], (LAYERS, F), 0.3, 4.0, (), jnp.float32),
        "mask_logits": bell_draw(splits[5], (LAYERS, SECTIONS, F), 1.0, 6.0, (), jnp.float32),
        "thresholds": jnp.clip(jax.random.uniform(splits[6], (LAYERS, SECTIONS), jnp.float32, 0.5, 2.5), 0.5, 2.5),
        "gate_in": bell_draw(splits[7], (LAYERS, SECTIONS, 2 * F, 2 * F), (2 * F) ** -0.5, 0.1875, ((2, 8),)),
        "bias_in": bell_draw(splits[8], (LAYERS, SECTIONS, 2 * F), 0.5, 4.0, (), jnp.float32),
        "gate_out": bell_draw(splits[9], (LAYERS, SECTIONS, 2 * F, F), (2 * F) ** -0.5, 0.1875, ((2, 8),)),
        "bias_out": bell_draw(splits[10], (LAYERS, SECTIONS, F), 0.5, 4.0, (), jnp.float32),
        "cotangent": bell_draw(splits[11], (ROWS, F), 1.0, 6.0, ((0, 32),)),
    }


epsilon = 1e-05

@jax.custom_vjp
def low(v):
    return lax.optimization_barrier(v.astype(jnp.bfloat16)).astype(jnp.float32)

@jax.custom_vjp
def low_back(v):
    return v

def low_keep(v):
    return (low(v), None)

def low_pass(kept, grad):
    return (grad,)

def back_keep(v):
    return (v, None)

def back_low(kept, grad):
    return (low(grad),)
low.defvjp(low_keep, low_pass)
low_back.defvjp(back_keep, back_low)

def highest(left_side, right_side):
    return jnp.dot(left_side, right_side, precision=lax.Precision.HIGHEST)

def feature_mask(logits, thresh):
    centred = logits - jnp.max(logits)
    weights = jnp.exp(centred) * jax.nn.softplus(centred + thresh)
    return weights / jnp.sum(weights)

def norm_rows(inputs, gain, shift, onehot, member):
    counts = lax.optimization_barrier(jnp.sum(member, axis=0))
    average = highest(member.T, inputs) / counts[:, None]
    centred = inputs - highest(onehot, average)
    spread = highest(member.T, centred * centred) / counts[:, None]
    scaling = lax.rsqrt(spread + epsilon)
    return centred * highest(onehot, scaling) * gain + shift

def section(hidden, normed, logits, thresh, weight_in, bias_in, weight_out, bias_out):
    columns = hidden.shape[1]
    masked = columns * feature_mask(logits, thresh) * normed
    first_in = low(jnp.concatenate([masked, hidden], axis=1))
    gate_pre = low_back(highest(first_in, weight_in) + bias_in)
    update = jax.nn.sigmoid(gate_pre[:, :columns])
    reset_gate = jax.nn.sigmoid(gate_pre[:, columns:])
    second_in = low(jnp.concatenate([reset_gate * hidden, normed], axis=1))
    candidate = jnp.tanh(low_back(highest(second_in, weight_out) + bias_out))
    return (1.0 - update) * hidden + update * candidate

def forward(inputs, gains, shifts, mask_logits, thresholds, gate_in, bias_in, gate_out, bias_out, onehot, member):
    current = inputs
    checked_section = jax.checkpoint(section)
    for layer_no in range(LAYERS):
        normed = norm_rows(current, gains[layer_no], shifts[layer_no], onehot, member)
        hidden = normed
        for section_no in range(SECTIONS):
            hidden = checked_section(hidden, normed, mask_logits[layer_no, section_no], thresholds[layer_no, section_no], gate_in[layer_no, section_no], bias_in[layer_no, section_no], gate_out[layer_no, section_no], bias_out[layer_no, section_no])
        current = current + hidden
    return current

def reference(features, row_valid, micro_batch, gains, shifts, mask_logits, thresholds, gate_in, bias_in, gate_out, bias_out, cotangent):
    valid_rows = row_valid.astype(jnp.float32)
    onehot = (micro_batch[:, None] == jnp.arange(MB, dtype=jnp.int32)[None, :]).astype(jnp.float32)
    member = onehot * valid_rows[:, None]
    forward_fn = functools.partial(forward, onehot=onehot, member=member)
    primals = (features.astype(jnp.float32), gains, shifts, mask_logits, thresholds, gate_in.astype(jnp.float32), bias_in, gate_out.astype(jnp.float32), bias_out)
    result, pullback = jax.vjp(forward_fn, *primals)
    gradients = pullback(cotangent.astype(jnp.float32) * valid_rows[:, None])
    return (result.astype(jnp.bfloat16), gradients[0], gradients[1], gradients[2], gradients[3], gradients[4], gradients[5], gradients[6], gradients[7], gradients[8])
```

```python
import functools

import jax
import jax.numpy as jnp
from jax import lax
from jax.experimental import pallas as pl
from jax.experimental.pallas import tpu as pltpu
from jax.sharding import PartitionSpec as P

SECTIONS = 6
LAYERS = 2
MB = 4
BF16 = jnp.bfloat16
F32 = jnp.float32
EPSILON = 1e-05
TILE = 256
VMEM_LIMIT = 60 * 1024 * 1024
GROUPS = (((0, 1), (1, 3), (3, 6)), ((0, 3), (3, 5), (5, 6)))


def gate(x):
    return 0.5 * jnp.tanh(0.5 * x) + 0.5


def load_weights(table, arrays, wbuf, sems, n, pr):
    for part, lo, hi in ((0, 0, 1), (1, 1, n)):
        if lo == hi:
            continue
        at = 0
        for array in arrays:
            for slot in range(array.shape[0]):
                row = pl.multiple_of(table[at], pr)
                pltpu.make_async_copy(
                    array.at[slot, pl.ds(lo, hi - lo)],
                    wbuf.at[pl.ds(lo, hi - lo), pl.ds(row, pr)],
                    sems.at[part],
                ).start()
                at += 1


def wait_weights(wbuf, sems, n, part):
    lo, hi = (0, 1) if part == 0 else (1, n)
    whole = wbuf.at[pl.ds(lo, hi - lo)]
    pltpu.make_async_copy(whole, whole, sems.at[part]).wait()


def forward_kernel(n, n_arrays, pr, tile, table, *refs):
    hidden_in, normed, mask, bias_in, bias_out = refs[:5]
    arrays = refs[5 : 5 + n_arrays]
    hidden_out, s_hidden, s_update, s_reset, s_cand = refs[5 + n_arrays : 10 + n_arrays]
    wbuf, hid, sems = refs[10 + n_arrays :]
    step = pl.program_id(0)
    rows, cols = hid.shape

    @pl.when(step == 0)
    def _():
        load_weights(table, arrays, wbuf, sems, n, pr)
        hid[...] = hidden_in[...]
        wait_weights(wbuf, sems, n, 0)

    if n > 1:
        @pl.when(step == 1)
        def _():
            wait_weights(wbuf, sems, n, 1)

    w = wbuf.at[step]
    mask_row = mask[0]
    b_in = bias_in[0]
    b_out = bias_out[0]

    def body(t, _):
        at = pl.ds(pl.multiple_of(t * tile, tile), tile)
        h = hid[at, :]
        x = normed[at, :]
        first_in = jnp.concatenate([(mask_row * x).astype(BF16), h.astype(BF16)], axis=1)
        pre = jnp.dot(first_in, w[:, : 2 * cols], preferred_element_type=F32) + b_in
        update = gate(pre[:, :cols])
        reset = gate(pre[:, cols:])
        second_in = jnp.concatenate([(reset * h).astype(BF16), x.astype(BF16)], axis=1)
        raw = jnp.dot(second_in, w[:, 2 * cols :], preferred_element_type=F32) + b_out
        cand = jnp.tanh(raw)
        s_hidden[0, at, :] = h.astype(s_hidden.dtype)
        s_update[0, at, :] = update.astype(s_update.dtype)
        s_reset[0, at, :] = reset.astype(s_reset.dtype)
        s_cand[0, at, :] = cand.astype(s_cand.dtype)
        hid[at, :] = h + update * (cand - h)
        return 0

    lax.fori_loop(0, rows // tile, body, 0)

    @pl.when(step == n - 1)
    def _():
        hidden_out[...] = hid[...]


def forward_chunk(table, hidden, normed, masks, bias_in, bias_out, arrays, tile=256, sdt=F32):
    n = masks.shape[0]
    rows, cols = hidden.shape
    pr = arrays[0].shape[2]
    depth = 2 * cols
    whole = pl.BlockSpec((rows, cols), lambda i, *_: (0, 0))
    row = lambda width: pl.BlockSpec((1, 1, width), lambda i, *_: (i, 0, 0))
    per = pl.BlockSpec((1, rows, cols), lambda i, *_: (i, 0, 0))
    saved = jax.ShapeDtypeStruct((n, rows, cols), sdt)
    return pl.pallas_call(
        functools.partial(forward_kernel, n, len(arrays), pr, tile),
        grid_spec=pltpu.PrefetchScalarGridSpec(
            num_scalar_prefetch=1,
            grid=(n,),
            in_specs=[whole, whole, row(cols), row(2 * cols), row(cols)] + [pl.BlockSpec(memory_space=pl.ANY)] * len(arrays),
            out_specs=[whole, per, per, per, per],
            scratch_shapes=[
                pltpu.VMEM((n, depth, 3 * cols), BF16),
                pltpu.VMEM((rows, cols), F32),
                pltpu.SemaphoreType.DMA((2,)),
            ],
        ),
        out_shape=[jax.ShapeDtypeStruct((rows, cols), F32)] + [saved] * 4,
        compiler_params=pltpu.CompilerParams(vmem_limit_bytes=VMEM_LIMIT),
        cost_estimate=pl.CostEstimate(
            flops=n * 2 * rows * depth * 3 * cols, bytes_accessed=n * (depth * 3 * cols * 2 + 16 * rows * cols), transcendentals=n * 3 * rows * cols
        ),
        name="forward_sections",
    )(table, hidden, normed, masks[:, None], bias_in[:, None], bias_out[:, None], *arrays)


def backward_kernel(n, n_in, n_out, pr, tile, table, *refs):
    gh_in, gn_in, normed, mask, s_hidden, s_update, s_reset, s_cand = refs[:8]
    arrays = refs[8 : 8 + n_in]
    gh_out, gn_out, g_mask, g_bin, g_bout = refs[8 + n_in : 13 + n_in]
    outs = refs[13 + n_in : 13 + n_in + n_out]
    wbuf, gh, gn, fi, si, gg, gr, stage, sems, out_sems = refs[13 + n_in + n_out :]
    step = pl.program_id(0)
    sec = n - 1 - step
    rows, cols = gh.shape
    wide = 2 * cols

    def wait_out(slot):
        whole = stage.at[slot]
        pltpu.make_async_copy(whole, whole, out_sems.at[slot]).wait()

    @pl.when(step == 0)
    def _():
        for part, lo, hi in ((0, n - 1, n), (1, 0, n - 1)):
            if lo == hi:
                continue
            at = 0
            for array in arrays:
                for slot in range(array.shape[0]):
                    row = pl.multiple_of(table[at], pr)
                    pltpu.make_async_copy(
                        array.at[slot, pl.ds(lo, hi - lo)],
                        wbuf.at[pl.ds(lo, hi - lo), pl.ds(row, pr)],
                        sems.at[part],
                    ).start()
                    at += 1
        gh[...] = gh_in[...]
        gn[...] = gn_in[...]
        whole = wbuf.at[pl.ds(n - 1, 1)]
        pltpu.make_async_copy(whole, whole, sems.at[0]).wait()

    if n > 1:
        @pl.when(step == 1)
        def _():
            whole = wbuf.at[pl.ds(0, n - 1)]
            pltpu.make_async_copy(whole, whole, sems.at[1]).wait()

    w = wbuf.at[sec]
    mask_row = mask[0]
    nt = (((1,), (1,)), ((), ()))
    tn = (((0,), (0,)), ((), ()))

    def body(t, sums):
        m_sum, bi_sum, bo_sum = sums
        at = pl.ds(pl.multiple_of(t * tile, tile), tile)
        g = gh[at, :]
        h = s_hidden[0, at, :].astype(F32)
        u = s_update[0, at, :].astype(F32)
        r = s_reset[0, at, :].astype(F32)
        c = s_cand[0, at, :].astype(F32)
        x = normed[at, :]
        grad_update = g * (c - h)
        grad_raw = (g * u * (1.0 - c * c)).astype(BF16)
        gr[at, :] = grad_raw
        si[at, :cols] = (r * h).astype(BF16)
        si[at, cols:] = x.astype(BF16)
        fi[at, :cols] = (mask_row * x).astype(BF16)
        fi[at, cols:] = h.astype(BF16)
        second = lax.dot_general(grad_raw, w[:, wide:], nt, preferred_element_type=F32)
        g2 = second[:, :cols]
        gates_u = (grad_update * u * (1.0 - u)).astype(BF16)
        gates_r = (g2 * h * r * (1.0 - r)).astype(BF16)
        gates = jnp.concatenate([gates_u, gates_r], axis=1)
        gg[at, :] = gates
        first = lax.dot_general(gates, w[:, :wide], nt, preferred_element_type=F32)
        gm = first[:, :cols]
        gn[at, :] = gn[at, :] + second[:, cols:] + gm * mask_row
        gh[at, :] = g * (1.0 - u) + g2 * r + first[:, cols:]
        m_sum = m_sum + jnp.sum(gm * x, axis=0, keepdims=True)
        bi_sum = bi_sum + jnp.sum(gates.astype(F32), axis=0, keepdims=True)
        bo_sum = bo_sum + jnp.sum(grad_raw.astype(F32), axis=0, keepdims=True)
        return m_sum, bi_sum, bo_sum

    zero = lambda width: jnp.zeros((1, width), F32)
    m_sum, bi_sum, bo_sum = lax.fori_loop(0, rows // tile, body, (zero(cols), zero(wide), zero(cols)))
    g_mask[0] = m_sum * float(cols)
    g_bin[0] = bi_sum
    g_bout[0] = bo_sum

    slot = lax.rem(step, 2)
    if n > 2:
        @pl.when(step >= 2)
        def _():
            wait_out(slot)

    mt = 256
    for m in range(0, wide, mt):
        stage[slot, m : m + mt, wide:] = lax.dot_general(si[:, m : m + mt], gr[...], tn, preferred_element_type=F32).astype(BF16)
        stage[slot, m : m + mt, :wide] = lax.dot_general(fi[:, m : m + mt], gg[...], tn, preferred_element_type=F32).astype(BF16)

    at = 0
    for out in outs:
        for s in range(out.shape[0]):
            row = pl.multiple_of(table[at], pr)
            pltpu.make_async_copy(stage.at[slot, pl.ds(row, pr)], out.at[s, sec], out_sems.at[slot]).start()
            at += 1

    @pl.when(step == n - 1)
    def _():
        gh_out[...] = gh[...]
        gn_out[...] = gn[...]
        if n > 1:
            wait_out(1 - slot)
        wait_out(slot)


def backward_chunk(table, gh, gn, normed, masks, saved, arrays, out_slots, tile=256):
    n = masks.shape[0]
    rows, cols = gh.shape
    pr = arrays[0].shape[2]
    depth = 2 * cols
    whole = pl.BlockSpec((rows, cols), lambda i, *_: (0, 0))
    row = lambda width: pl.BlockSpec((1, 1, width), lambda i, *_: (n - 1 - i, 0, 0))
    per = pl.BlockSpec((1, rows, cols), lambda i, *_: (n - 1 - i, 0, 0))
    any_spec = pl.BlockSpec(memory_space=pl.ANY)
    state = jax.ShapeDtypeStruct((rows, cols), F32)
    vec = lambda width: jax.ShapeDtypeStruct((n, 1, width), F32)
    results = pl.pallas_call(
        functools.partial(backward_kernel, n, len(arrays), len(out_slots), pr, tile),
        grid_spec=pltpu.PrefetchScalarGridSpec(
            num_scalar_prefetch=1,
            grid=(n,),
            in_specs=[whole, whole, whole, row(cols), per, per, per, per] + [any_spec] * len(arrays),
            out_specs=[whole, whole, row(cols), row(depth), row(cols)] + [any_spec] * len(out_slots),
            scratch_shapes=[
                pltpu.VMEM((n, depth, 3 * cols), BF16),
                pltpu.VMEM((rows, cols), F32),
                pltpu.VMEM((rows, cols), F32),
                pltpu.VMEM((rows, depth), BF16),
                pltpu.VMEM((rows, depth), BF16),
                pltpu.VMEM((rows, depth), BF16),
                pltpu.VMEM((rows, cols), BF16),
                pltpu.VMEM((2, depth, 3 * cols), BF16),
                pltpu.SemaphoreType.DMA((2,)),
                pltpu.SemaphoreType.DMA((2,)),
            ],
        ),
        out_shape=[state, state, vec(cols), vec(depth), vec(cols)]
        + [jax.ShapeDtypeStruct((s, n, pr, 3 * cols), BF16) for s in out_slots],
        compiler_params=pltpu.CompilerParams(vmem_limit_bytes=VMEM_LIMIT),
        cost_estimate=pl.CostEstimate(
            flops=n * 4 * rows * depth * 3 * cols, bytes_accessed=n * (depth * 3 * cols * 4 + 16 * rows * cols), transcendentals=0
        ),
        name="backward_sections",
    )(table, gh, gn, normed, masks[:, None], *saved, *arrays)
    gh, gn, g_mask, g_bin, g_bout = results[:5]
    return gh, gn, g_mask[:, 0], g_bin[:, 0], g_bout[:, 0], results[5:]


def pick(micro, table):
    out = table[MB - 1 : MB, :]
    for b in range(MB - 2, -1, -1):
        out = jnp.where(micro == b, table[b : b + 1, :], out)
    return out


def stats_kernel(with_hidden, *refs):
    if with_hidden:
        u_ref, hidden_ref, micro_ref, valid_ref, out_ref, stats_ref = refs
        u = u_ref[...] + hidden_ref[...]
        out_ref[...] = u
    else:
        u_ref, micro_ref, valid_ref, stats_ref = refs
        u = u_ref[...].astype(F32)
    micro = micro_ref[...]
    valid = valid_ref[...]
    width = u.shape[1]
    counts, means = [], []
    for b in range(MB):
        member = jnp.where(micro == b, valid, 0.0)
        count = jnp.sum(member)
        total = jnp.sum(u * member, axis=0, keepdims=True)
        counts.append(jnp.full((1, width), count, F32))
        means.append(total / jnp.maximum(count, 1.0))
    centred = u - pick(micro, jnp.concatenate(means, axis=0))
    squares = centred * centred * valid
    for b in range(MB):
        stats_ref[b : b + 1, :] = counts[b]
        stats_ref[MB + b : MB + b + 1, :] = means[b]
        stats_ref[2 * MB + b : 2 * MB + b + 1, :] = jnp.sum(jnp.where(micro == b, squares, 0.0), axis=0, keepdims=True)


def local_stats(u, hidden, micro, valid):
    rows, cols = u.shape
    stats = jax.ShapeDtypeStruct((3 * MB, cols), F32)
    args = (u, micro, valid) if hidden is None else (u, hidden, micro, valid)
    out = [stats] if hidden is None else [jax.ShapeDtypeStruct((rows, cols), F32), stats]
    res = pl.pallas_call(
        functools.partial(stats_kernel, hidden is not None),
        out_shape=out,
        compiler_params=pltpu.CompilerParams(vmem_limit_bytes=VMEM_LIMIT),
        cost_estimate=pl.CostEstimate(flops=20 * rows * cols, bytes_accessed=8 * rows * cols, transcendentals=0),
        name="local_stats",
    )(*args)
    return (None, res[0]) if hidden is None else res


def merge_stats(a, b):
    na, ma, qa = a[:MB], a[MB : 2 * MB], a[2 * MB :]
    nb, mb, qb = b[:MB], b[MB : 2 * MB], b[2 * MB :]
    n = na + nb
    inverse = 1.0 / jnp.maximum(n, 1.0)
    apart = ma - mb
    return jnp.concatenate([n, (na * ma + nb * mb) * inverse, qa + qb + apart * apart * (na * nb * inverse)], axis=0)


def norm_kernel(u_ref, micro_ref, stats_ref, gain_ref, shift_ref, normed_ref):
    stats = stats_ref[...]
    scale = lax.rsqrt(stats[2 * MB :] / stats[:MB] + EPSILON)
    micro = micro_ref[...]
    standard = (u_ref[...].astype(F32) - pick(micro, stats[MB : 2 * MB])) * pick(micro, scale)
    normed_ref[...] = standard * gain_ref[...] + shift_ref[...]


def norm_rows(u, micro, stats, gain, shift):
    rows, cols = u.shape
    return pl.pallas_call(
        norm_kernel,
        out_shape=jax.ShapeDtypeStruct((rows, cols), F32),
        compiler_params=pltpu.CompilerParams(vmem_limit_bytes=VMEM_LIMIT),
        cost_estimate=pl.CostEstimate(flops=20 * rows * cols, bytes_accessed=8 * rows * cols, transcendentals=0),
        name="norm_rows",
    )(u, micro, stats, gain[None], shift[None])


def pool_kernel(u_ref, micro_ref, stats_ref, gn_ref, gh_ref, total_ref, pooled_ref):
    stats = stats_ref[...]
    scale = lax.rsqrt(stats[2 * MB :] / stats[:MB] + EPSILON)
    micro = micro_ref[...]
    standard = (u_ref[...].astype(F32) - pick(micro, stats[MB : 2 * MB])) * pick(micro, scale)
    total = gn_ref[...] + gh_ref[...]
    total_ref[...] = total
    product = total * standard
    for b in range(MB):
        pooled_ref[b : b + 1, :] = jnp.sum(jnp.where(micro == b, total, 0.0), axis=0, keepdims=True)
        pooled_ref[MB + b : MB + b + 1, :] = jnp.sum(jnp.where(micro == b, product, 0.0), axis=0, keepdims=True)


def pool_grads(u, micro, stats, gn, gh):
    rows, cols = u.shape
    return pl.pallas_call(
        pool_kernel,
        out_shape=[jax.ShapeDtypeStruct((rows, cols), F32), jax.ShapeDtypeStruct((2 * MB, cols), F32)],
        compiler_params=pltpu.CompilerParams(vmem_limit_bytes=VMEM_LIMIT),
        cost_estimate=pl.CostEstimate(flops=20 * rows * cols, bytes_accessed=16 * rows * cols, transcendentals=0),
        name="pool_grads",
    )(u, micro, stats, gn, gh)


def carry_kernel(u_ref, micro_ref, valid_ref, stats_ref, gain_ref, total_ref, pooled_ref, carried_ref, out_ref):
    stats = stats_ref[...]
    gain = gain_ref[...]
    counts = stats[:MB]
    scale = lax.rsqrt(stats[2 * MB :] / counts + EPSILON)
    pooled = pooled_ref[...]
    micro = micro_ref[...]
    row_scale = pick(micro, scale)
    standard = (u_ref[...].astype(F32) - pick(micro, stats[MB : 2 * MB])) * row_scale
    shift_term = pick(micro, gain * pooled[:MB] / counts)
    scale_term = pick(micro, gain * pooled[MB:] / counts)
    out_ref[...] = carried_ref[...] + row_scale * (
        total_ref[...] * gain - valid_ref[...] * (shift_term + standard * scale_term)
    )


def carry_grads(u, micro, valid, stats, gain, total, pooled, carried):
    rows, cols = u.shape
    return pl.pallas_call(
        carry_kernel,
        out_shape=jax.ShapeDtypeStruct((rows, cols), F32),
        compiler_params=pltpu.CompilerParams(vmem_limit_bytes=VMEM_LIMIT),
        cost_estimate=pl.CostEstimate(flops=30 * rows * cols, bytes_accessed=16 * rows * cols, transcendentals=0),
        name="carry_grads",
    )(u, micro, valid, stats, gain[None], total, pooled, carried)


def feature_mask(logits, thresh):
    centred = logits - jnp.max(logits)
    weights = jnp.exp(centred) * jax.nn.softplus(centred + thresh)
    return weights / jnp.sum(weights)


def along(axis, size, flip):
    return [(i, i ^ flip) for i in range(size)]


class CubeTransfers:
    def __init__(self, dp_size, fsdp_size):
        self.dp_size, self.fsdp_size = dp_size, fsdp_size
        self.slots = [4, 4, 4, 2, 2, 16]

    def core(self, v):
        return lax.ppermute(v, "dp", along("dp", self.dp_size, 1))

    def x(self, v):
        return lax.ppermute(v, "dp", along("dp", self.dp_size, 2))

    def y(self, v):
        return lax.ppermute(v, "fsdp", along("fsdp", self.fsdp_size, 1))

    def z(self, v, flip):
        return lax.ppermute(v, "fsdp", along("fsdp", self.fsdp_size, 2 * flip))

    def all_reduce(self, v, merge):
        for step in (self.core, self.x, self.y, lambda a: self.z(a, 1), lambda a: self.z(a, 2)):
            v = merge(v, step(v))
        return v

    def table(self, shard_rows):
        q = lax.axis_index("dp").astype(jnp.int32)
        f = lax.axis_index("fsdp").astype(jnp.int32)
        rows = []
        for core in (0, 1):
            for flip_q, flip_y, slots in ((0, 0, range(4)), (0, 1, range(4)), (2, 0, range(4)), (2, 1, range(4))):
                for j in slots:
                    place = f ^ (2 * j + flip_y)
                    rows.append(place * shard_rows + (q ^ (flip_q + core)) * (shard_rows // self.dp_size))
        return jnp.stack(rows)

    def gather(self, shard):
        rows = shard.shape[1] // self.dp_size
        own = lax.dynamic_slice_in_dim(shard, lax.axis_index("dp") * rows, rows, axis=1)
        held = jnp.stack([own] + [self.z(own, j) for j in (1, 2, 3)])
        by_y, by_x = self.y(held), self.x(held)
        far_x, far_y = self.x(by_y[:2]), self.y(by_x[2:])
        mine = [held, by_y, by_x, far_x, far_y]
        return mine + [self.core(v) for v in mine]

    def scatter(self, parts):
        held, by_y, by_x, far_x, far_y, other = parts
        other = self.core(other)
        add = lambda *vs: sum(v.astype(F32) for v in vs)
        low = lambda v: v.astype(BF16)
        far_x = low(add(far_x, other[12:14]))
        far_y = low(add(far_y, other[14:16]))
        got_x, got_y = self.x(far_x), self.y(far_y)
        by_y = low(jnp.concatenate([add(by_y[:2], other[4:6], got_x), add(by_y[2:], other[6:8])]))
        by_x = low(jnp.concatenate([add(by_x[:2], other[8:10]), add(by_x[2:], other[10:12], got_y)]))
        got_y, got_x = self.y(by_y), self.x(by_x)
        sums = [low(add(held[j], other[j], got_y[j], got_x[j])) for j in range(4)]
        got = [self.z(sums[j], j) for j in (1, 2, 3)]
        own = low(add(sums[0], *got))
        by_x = self.x(own)
        return [own, self.core(own), by_x, self.core(by_x)]

    def pieces_table(self, shard_rows):
        q = lax.axis_index("dp").astype(jnp.int32)
        return jnp.stack([(q ^ j) * (shard_rows // self.dp_size) for j in range(4)])


class PlainTransfers:
    def __init__(self, dp_size, fsdp_size):
        self.fsdp_size = fsdp_size
        self.slots = [fsdp_size]

    def all_reduce(self, v, merge):
        every = lax.all_gather(v, ("dp", "fsdp"))
        while every.shape[0] > 1:
            half = every.shape[0] // 2
            every = jax.vmap(merge)(every[:half], every[half:])
        return every[0]

    def table(self, shard_rows):
        return jnp.arange(self.fsdp_size, dtype=jnp.int32) * shard_rows

    def gather(self, shard):
        return [lax.all_gather(shard, "fsdp")]

    def scatter(self, parts):
        own = lax.psum_scatter(parts[0], "fsdp", scatter_dimension=0)
        return [lax.psum(own, "dp")]

    def pieces_table(self, shard_rows):
        return jnp.zeros((1,), jnp.int32)


def place_kernel(n_pieces, first, table, *refs):
    pieces = refs[:n_pieces]
    g_in, g_out = refs[-2:]
    pr = pieces[0].shape[1]
    wide = g_in.shape[-1]
    for piece, j in zip(pieces, range(n_pieces)):
        row = pl.multiple_of(table[j], pr)
        value = piece[0].astype(F32)
        g_in[0, 0, pl.ds(row, pr), :] = value[:, :wide]
        g_out[0, 0, pl.ds(row, pr), :] = value[:, wide:]


def place_grads(table, pieces, layer, start, shard_rows, previous):
    n, pr, width = pieces[0].shape
    wide = 2 * width // 3
    shapes = [
        jax.ShapeDtypeStruct((LAYERS, SECTIONS, shard_rows, wide), F32),
        jax.ShapeDtypeStruct((LAYERS, SECTIONS, shard_rows, width - wide), F32),
    ]
    block = lambda w: pl.BlockSpec((1, 1, shard_rows, w), lambda i, *_: (layer, start + i, 0, 0))
    n_pieces = len(pieces)
    extra = [] if previous is None else list(previous)
    return pl.pallas_call(
        functools.partial(place_kernel, n_pieces, previous is None),
        grid_spec=pltpu.PrefetchScalarGridSpec(
            num_scalar_prefetch=1,
            grid=(n,),
            in_specs=[pl.BlockSpec((1, pr, width), lambda i, *_: (i, 0, 0))] * n_pieces
            + [pl.BlockSpec(memory_space=pl.ANY)] * len(extra),
            out_specs=[block(wide), block(width - wide)],
        ),
        out_shape=shapes,
        input_output_aliases={} if previous is None else {1 + n_pieces: 0, 2 + n_pieces: 1},
        cost_estimate=pl.CostEstimate(flops=0, bytes_accessed=n * shard_rows * width * 6, transcendentals=0),
        name="place_grads",
    )(table, *pieces, *extra)


def local(
    moves,
    features,
    row_valid,
    micro_batch,
    gains,
    shifts,
    mask_logits,
    thresholds,
    gate_in,
    bias_in,
    gate_out,
    bias_out,
    cotangent,
):
    columns = features.shape[1]
    shard_rows = gate_in.shape[2]
    valid = row_valid.astype(F32)[:, None]
    micro = micro_batch[:, None]
    table = moves.table(shard_rows)
    weights = [
        [
            moves.gather(jnp.concatenate([gate_in[layer, lo:hi], gate_out[layer, lo:hi]], axis=-1))
            for lo, hi in GROUPS[layer]
        ]
        for layer in range(LAYERS)
    ]
    masks = columns * jax.vmap(jax.vmap(feature_mask))(mask_logits, thresholds)
    add = lambda a, b: a + b

    current = features
    hidden = None
    records = []
    for layer in range(LAYERS):
        summed, stats = local_stats(current, hidden, micro, valid)
        current = current if summed is None else summed
        stats = moves.all_reduce(stats, merge_stats)
        normed = norm_rows(current, micro, stats, gains[layer], shifts[layer])
        hidden = normed
        stored = []
        for (lo, hi), arrays in zip(GROUPS[layer], weights[layer]):
            hidden, *saved = forward_chunk(
                table, hidden, normed, masks[layer, lo:hi], bias_in[layer, lo:hi], bias_out[layer, lo:hi], arrays
            )
            stored.append(saved)
        records.append((current, stats, normed, stored))
    mixed_out = (current + hidden).astype(BF16)

    carried = cotangent.astype(F32) * valid
    pieces_table = moves.pieces_table(shard_rows)
    grads = None
    sums = [None] * LAYERS
    pooled_of = [None] * LAYERS
    for layer in reversed(range(LAYERS)):
        current, stats, normed, stored = records[layer]
        gh = carried
        gn = jnp.zeros_like(carried)
        parts = []
        for (lo, hi), arrays, saved in reversed(list(zip(GROUPS[layer], weights[layer], stored))):
            gh, gn, g_mask, g_bin, g_bout, out = backward_chunk(
                table, gh, gn, normed, masks[layer, lo:hi], saved, arrays, moves.slots
            )
            parts.append((g_mask, g_bin, g_bout))
            grads = place_grads(pieces_table, moves.scatter(out), layer, lo, shard_rows, grads)
        total, pooled = pool_grads(current, micro, stats, gn, gh)
        vectors = jnp.concatenate([jnp.concatenate(p, axis=1) for p in reversed(parts)], axis=0)
        if layer == 0:
            both = moves.all_reduce(jnp.concatenate([pooled, vectors.reshape(-1, columns)]), add)
            pooled = both[: 2 * MB]
            vectors = both[2 * MB :].reshape(vectors.shape)
        else:
            pooled = moves.all_reduce(pooled, add)
            vectors = moves.all_reduce(vectors, add)
        sums[layer] = vectors
        pooled_of[layer] = pooled
        carried = carry_grads(current, micro, valid, stats, gains[layer], total, pooled, carried)
    stacked = jnp.stack(sums)
    pooled = jnp.stack(pooled_of)
    _, mask_pull = jax.vjp(jax.vmap(jax.vmap(feature_mask)), mask_logits, thresholds)
    grad_logits, grad_thresholds = mask_pull(stacked[..., :columns])
    return (
        mixed_out,
        carried,
        jnp.sum(pooled[:, MB:], axis=1),
        jnp.sum(pooled[:, :MB], axis=1),
        grad_logits,
        grad_thresholds,
        grads[0],
        stacked[..., columns : 3 * columns],
        grads[1],
        stacked[..., 3 * columns :],
    )


def solution(mesh):
    rows = P(("dp", "fsdp"), None)
    row = P(("dp", "fsdp"))
    shard = P(None, None, "fsdp", None)
    in_specs = (rows, row, row, P(), P(), P(), P(), shard, P(), shard, P(), rows)
    out_specs = (rows, rows, P(), P(), P(), P(), shard, P(), shard, P())
    dp_size, fsdp_size = mesh.shape["dp"], mesh.shape["fsdp"]
    kind = CubeTransfers if (dp_size, fsdp_size) == (4, 8) else PlainTransfers
    return jax.shard_map(
        functools.partial(local, kind(dp_size, fsdp_size)),
        mesh=mesh,
        in_specs=in_specs,
        out_specs=out_specs,
        check_vma=False,
    )
```

```python
import functools

import jax
import jax.numpy as jnp
from jax import lax
from jax.experimental import pallas as pl
from jax.experimental.pallas import tpu as pltpu
from jax.sharding import PartitionSpec as P

SECTIONS = 6
LAYERS = 2
MB = 4
BF16 = jnp.bfloat16
F32 = jnp.float32
EPSILON = 1e-05
TILE = 256
COST = pl.CostEstimate(flops=1, bytes_accessed=1, transcendentals=0)
LONG = pl.CostEstimate(flops=2 * 10**10, bytes_accessed=1, transcendentals=0)
VMEM_LIMIT = 60 * 1024 * 1024
GATHERS = ((0, 3), (3, 6), (6, 12))
GROUPS = ((0, 3), (3, 6), (6, 9), (9, 12))
RING_SUM = (6, 12)


def gate(x):
    return 0.5 * jnp.tanh(0.5 * x) + 0.5


def load_weights(table, arrays, wbuf, sems, n, pr, first):
    for part, lo, hi in ((0, 0, 1), (1, 1, n)):
        if lo == hi:
            continue
        at = 0
        for array in arrays:
            for slot in range(array.shape[0]):
                row = pl.multiple_of(table[at], pr)
                pltpu.make_async_copy(
                    array.at[slot, pl.ds(first + lo, hi - lo)],
                    wbuf.at[pl.ds(lo, hi - lo), pl.ds(row, pr)],
                    sems.at[part],
                ).start()
                at += 1


def wait_weights(wbuf, sems, n, part):
    lo, hi = (0, 1) if part == 0 else (1, n)
    whole = wbuf.at[pl.ds(lo, hi - lo)]
    pltpu.make_async_copy(whole, whole, sems.at[part]).wait()


def forward_kernel(n, first, n_arrays, n_tokens, pr, tile, table, *refs):
    hidden_in, normed, mask, bias_in, bias_out = refs[:5]
    arrays = refs[5 : 5 + n_arrays]
    refs = refs[n_tokens:]
    hidden_out = refs[5 + n_arrays]
    factors = refs[6 + n_arrays : 11 + n_arrays]
    h_turned, rh_turned = refs[11 + n_arrays : 13 + n_arrays]
    wbuf, hid, sems = refs[13 + n_arrays :]
    step = pl.program_id(0)
    rows, cols = hid.shape

    @pl.when(step == 0)
    def _():
        load_weights(table, arrays, wbuf, sems, n, pr, first)
        hid[...] = hidden_in[...]
        wait_weights(wbuf, sems, n, 0)

    if n > 1:
        @pl.when(step == 1)
        def _():
            wait_weights(wbuf, sems, n, 1)

    w = wbuf.at[step]
    mask_row = mask[0]
    b_in = bias_in[0]
    b_out = bias_out[0]

    for t in range(rows // tile):
        at = slice(t * tile, (t + 1) * tile)
        h = hid[at, :]
        x = normed[at, :]
        low_h = h.astype(BF16)
        first_in = jnp.concatenate([(mask_row * x).astype(BF16), low_h], axis=1)
        pre = jnp.dot(first_in, w[:, : 2 * cols], preferred_element_type=F32) + b_in
        update = gate(pre[:, :cols])
        reset = gate(pre[:, cols:])
        low_rh = (reset * h).astype(BF16)
        second_in = jnp.concatenate([low_rh, x.astype(BF16)], axis=1)
        raw = jnp.dot(second_in, w[:, 2 * cols :], preferred_element_type=F32) + b_out
        cand = jnp.tanh(raw)
        keep = 1.0 - update
        apart = cand - h
        hid[at, :] = h + update * apart
        values = (update * (1.0 - cand * cand), apart * update * keep, h * reset * (1.0 - reset), keep, reset)
        for ref, value in zip(factors, values):
            ref[0, at, :] = value.astype(ref.dtype)
        h_turned[0, :, at] = low_h.T
        rh_turned[0, :, at] = low_rh.T

    @pl.when(step == n - 1)
    def _():
        hidden_out[...] = hid[...]


def forward_chunk(table, hidden, normed, masks, bias_in, bias_out, arrays, first, tokens=(), tile=TILE):
    n = masks.shape[0]
    rows, cols = hidden.shape
    pr = arrays[0].shape[2]
    depth = 2 * cols
    whole = pl.BlockSpec((rows, cols), lambda i, *_: (0, 0))
    row = lambda width: pl.BlockSpec((1, 1, width), lambda i, *_: (i, 0, 0))
    per = pl.BlockSpec((1, rows, cols), lambda i, *_: (i, 0, 0))
    turned = pl.BlockSpec((1, cols, rows), lambda i, *_: (i, 0, 0))
    saved = [jax.ShapeDtypeStruct((n, rows, cols), t) for t in (F32,) * 5] + [jax.ShapeDtypeStruct((n, cols, rows), BF16)] * 2
    return pl.pallas_call(
        functools.partial(forward_kernel, n, first, len(arrays), len(tokens), pr, tile),
        grid_spec=pltpu.PrefetchScalarGridSpec(
            num_scalar_prefetch=1,
            grid=(n,),
            in_specs=[whole, whole, row(cols), row(2 * cols), row(cols)] + [pl.BlockSpec(memory_space=pl.ANY)] * (len(arrays) + len(tokens)),
            out_specs=[whole] + [per] * 5 + [turned] * 2,
            scratch_shapes=[
                pltpu.VMEM((n, depth, 3 * cols), BF16),
                pltpu.VMEM((rows, cols), F32),
                pltpu.SemaphoreType.DMA((2,)),
            ],
        ),
        out_shape=[jax.ShapeDtypeStruct((rows, cols), F32)] + saved,
        compiler_params=pltpu.CompilerParams(vmem_limit_bytes=VMEM_LIMIT),
        cost_estimate=LONG,
        name="forward_sections",
    )(table, hidden, normed, masks[:, None], bias_in[:, None], bias_out[:, None], *arrays, *tokens)


def backward_kernel(n, first, n_in, n_out, n_tokens, pr, tile, table, *refs):
    gh_in, normed, x_turned, mask, mask_column = refs[:5]
    factors = refs[5:10]
    h_turned, rh_turned = refs[10:12]
    arrays = refs[12 : 12 + n_in]
    refs = refs[12 + n_in + n_tokens :]
    gh_out, gn_out, g_mask, g_bin, g_bout = refs[:5]
    outs = refs[5 : 5 + n_out]
    wbuf, gh, gn, gg, gr, stage, sems, out_sems = refs[5 + n_out :]
    step = pl.program_id(0)
    sec = n - 1 - step
    rows, cols = gh.shape
    wide = 2 * cols

    def wait_out(slot):
        whole = stage.at[slot]
        pltpu.make_async_copy(whole, whole, out_sems.at[slot]).wait()

    @pl.when(step == 0)
    def _():
        for part, lo, hi in ((0, n - 1, n), (1, 0, n - 1)):
            if lo == hi:
                continue
            at = 0
            for array in arrays:
                for slot in range(array.shape[0]):
                    row = pl.multiple_of(table[at], pr)
                    pltpu.make_async_copy(
                        array.at[slot, pl.ds(first + lo, hi - lo)],
                        wbuf.at[pl.ds(lo, hi - lo), pl.ds(row, pr)],
                        sems.at[part],
                    ).start()
                    at += 1
        gh[...] = gh_in[...]
        gn[...] = jnp.zeros_like(gn)
        whole = wbuf.at[pl.ds(n - 1, 1)]
        pltpu.make_async_copy(whole, whole, sems.at[0]).wait()

    if n > 1:
        @pl.when(step == 1)
        def _():
            whole = wbuf.at[pl.ds(0, n - 1)]
            pltpu.make_async_copy(whole, whole, sems.at[1]).wait()

    w = wbuf.at[sec]
    mask_row = mask[0]
    nt = (((1,), (1,)), ((), ()))

    m_sum = jnp.zeros((1, cols), F32)
    bi_sum = jnp.zeros((1, wide), F32)
    bo_sum = jnp.zeros((1, cols), F32)
    for t in range(rows // tile):
        at = slice(t * tile, (t + 1) * tile)
        g = gh[at, :]
        by_raw, by_update, by_reset, keep, reset = (ref[0, at, :].astype(F32) for ref in factors)
        grad_raw = (g * by_raw).astype(BF16)
        gr[at, :] = grad_raw
        second = lax.dot_general(grad_raw, w[:, wide:], nt, preferred_element_type=F32)
        g2 = second[:, :cols]
        gates = jnp.concatenate([(g * by_update).astype(BF16), (g2 * by_reset).astype(BF16)], axis=1)
        gg[at, :] = gates
        first = lax.dot_general(gates, w[:, :wide], nt, preferred_element_type=F32)
        gm = first[:, :cols]
        gn[at, :] = gn[at, :] + second[:, cols:] + gm * mask_row
        gh[at, :] = g * keep + g2 * reset + first[:, cols:]
        m_sum = m_sum + jnp.sum(gm * normed[at, :], axis=0, keepdims=True)
        bi_sum = bi_sum + jnp.sum(gates.astype(F32), axis=0, keepdims=True)
        bo_sum = bo_sum + jnp.sum(grad_raw.astype(F32), axis=0, keepdims=True)
    g_mask[0] = m_sum * float(cols)
    g_bin[0] = bi_sum
    g_bout[0] = bo_sum

    slot = lax.rem(step, 2)
    if n > 2:
        @pl.when(step >= 2)
        def _():
            wait_out(slot)

    stage[slot, :cols, wide:] = jnp.dot(rh_turned[0], gr[...], preferred_element_type=F32).astype(BF16)
    stage[slot, cols:, wide:] = jnp.dot(x_turned[...], gr[...], preferred_element_type=F32).astype(BF16)
    masked = jnp.dot(x_turned[...], gg[...], preferred_element_type=F32)
    stage[slot, :cols, :wide] = (masked * mask_column[0]).astype(BF16)
    stage[slot, cols:, :wide] = jnp.dot(h_turned[0], gg[...], preferred_element_type=F32).astype(BF16)

    at = sum(array.shape[0] for array in arrays)
    for out in outs:
        for s in range(out.shape[0]):
            row = pl.multiple_of(table[at], pr)
            pltpu.make_async_copy(stage.at[slot, pl.ds(row, pr)], out.at[s, sec], out_sems.at[slot]).start()
            at += 1

    @pl.when(step == n - 1)
    def _():
        gh_out[...] = gh[...]
        gn_out[...] = gn[...]
        if n > 1:
            wait_out(1 - slot)
        wait_out(slot)


def backward_chunk(table, gh, normed, x_turned, masks, saved, first_saved, arrays, first, out_slots, tokens=(), tile=TILE):
    n = masks.shape[0]
    rows, cols = gh.shape
    pr = arrays[0].shape[2]
    depth = 2 * cols
    whole = pl.BlockSpec((rows, cols), lambda i, *_: (0, 0))
    row = lambda width: pl.BlockSpec((1, 1, width), lambda i, *_: (n - 1 - i, 0, 0))
    turned = pl.BlockSpec((1, cols, rows), lambda i, *_: (first_saved + n - 1 - i, 0, 0))
    per = pl.BlockSpec((1, rows, cols), lambda i, *_: (first_saved + n - 1 - i, 0, 0))
    column = pl.BlockSpec((1, cols, 1), lambda i, *_: (n - 1 - i, 0, 0))
    any_spec = pl.BlockSpec(memory_space=pl.ANY)
    state = jax.ShapeDtypeStruct((rows, cols), F32)
    vec = lambda width: jax.ShapeDtypeStruct((n, 1, width), F32)
    results = pl.pallas_call(
        functools.partial(backward_kernel, n, first, len(arrays), len(out_slots), len(tokens), pr, tile),
        grid_spec=pltpu.PrefetchScalarGridSpec(
            num_scalar_prefetch=1,
            grid=(n,),
            in_specs=[whole, whole, pl.BlockSpec((cols, rows), lambda i, *_: (0, 0)), row(cols), column]
            + [per] * 5
            + [turned] * 2
            + [any_spec] * (len(arrays) + len(tokens)),
            out_specs=[whole, whole, row(cols), row(depth), row(cols)] + [any_spec] * len(out_slots),
            scratch_shapes=[
                pltpu.VMEM((n, depth, 3 * cols), BF16),
                pltpu.VMEM((rows, cols), F32),
                pltpu.VMEM((rows, cols), F32),
                pltpu.VMEM((rows, depth), BF16),
                pltpu.VMEM((rows, cols), BF16),
                pltpu.VMEM((2, depth, 3 * cols), BF16),
                pltpu.SemaphoreType.DMA((2,)),
                pltpu.SemaphoreType.DMA((2,)),
            ],
        ),
        out_shape=[state, state, vec(cols), vec(depth), vec(cols)]
        + [jax.ShapeDtypeStruct((s, n, pr, 3 * cols), BF16) for s in out_slots],
        compiler_params=pltpu.CompilerParams(vmem_limit_bytes=VMEM_LIMIT),
        cost_estimate=LONG,
        name="backward_sections",
    )(table, gh, normed, x_turned, masks[:, None], masks[:, :, None], *saved, *arrays, *tokens)
    gh, gn, g_mask, g_bin, g_bout = results[:5]
    return gh, gn, g_mask[:, 0], g_bin[:, 0], g_bout[:, 0], results[5:]


def pick(micro, table):
    out = table[MB - 1 : MB, :]
    for b in range(MB - 2, -1, -1):
        out = jnp.where(micro == b, table[b : b + 1, :], out)
    return out


def stats_kernel(with_hidden, n_tokens, *refs):
    if with_hidden:
        refs = refs[:4] + refs[4 + n_tokens :]
        u_ref, hidden_ref, micro_ref, valid_ref, out_ref, stats_ref = refs
        u = u_ref[...] + hidden_ref[...]
        out_ref[...] = u
    else:
        u_ref, micro_ref, valid_ref, stats_ref = refs
        u = u_ref[...].astype(F32)
    micro = micro_ref[...]
    valid = valid_ref[...]
    width = u.shape[1]
    counts, means = [], []
    for b in range(MB):
        member = jnp.where(micro == b, valid, 0.0)
        count = jnp.sum(member)
        total = jnp.sum(u * member, axis=0, keepdims=True)
        counts.append(jnp.full((1, width), count, F32))
        means.append(total / jnp.maximum(count, 1.0))
    centred = u - pick(micro, jnp.concatenate(means, axis=0))
    squares = centred * centred * valid
    for b in range(MB):
        stats_ref[b : b + 1, :] = counts[b]
        stats_ref[MB + b : MB + b + 1, :] = means[b]
        stats_ref[2 * MB + b : 2 * MB + b + 1, :] = jnp.sum(jnp.where(micro == b, squares, 0.0), axis=0, keepdims=True)


def local_stats(u, hidden, micro, valid, tokens=()):
    rows, cols = u.shape
    stats = jax.ShapeDtypeStruct((3 * MB, cols), F32)
    args = (u, micro, valid) if hidden is None else (u, hidden, micro, valid)
    out = [stats] if hidden is None else [jax.ShapeDtypeStruct((rows, cols), F32), stats]
    res = pl.pallas_call(
        functools.partial(stats_kernel, hidden is not None, len(tokens)),
        in_specs=[pl.BlockSpec(memory_space=pltpu.VMEM)] * len(args) + [pl.BlockSpec(memory_space=pl.ANY)] * len(tokens),
        out_shape=out,
        compiler_params=pltpu.CompilerParams(vmem_limit_bytes=VMEM_LIMIT),
        cost_estimate=COST,
        name="local_stats",
    )(*args, *tokens)
    return (None, res[0]) if hidden is None else res


def merge_stats(a, b):
    na, ma, qa = a[:MB], a[MB : 2 * MB], a[2 * MB :]
    nb, mb, qb = b[:MB], b[MB : 2 * MB], b[2 * MB :]
    n = na + nb
    inverse = 1.0 / jnp.maximum(n, 1.0)
    apart = ma - mb
    return jnp.concatenate([n, (na * ma + nb * mb) * inverse, qa + qb + apart * apart * (na * nb * inverse)], axis=0)


def norm_kernel(u_ref, micro_ref, stats_ref, gain_ref, shift_ref, normed_ref, turned_ref):
    stats = stats_ref[...]
    scale = lax.rsqrt(stats[2 * MB :] / stats[:MB] + EPSILON)
    micro = micro_ref[...]
    standard = (u_ref[...].astype(F32) - pick(micro, stats[MB : 2 * MB])) * pick(micro, scale)
    normed = standard * gain_ref[...] + shift_ref[...]
    normed_ref[...] = normed
    turned_ref[...] = normed.astype(BF16).T


def norm_rows(u, micro, stats, gain, shift):
    rows, cols = u.shape
    return pl.pallas_call(
        norm_kernel,
        out_shape=[jax.ShapeDtypeStruct((rows, cols), F32), jax.ShapeDtypeStruct((cols, rows), BF16)],
        compiler_params=pltpu.CompilerParams(vmem_limit_bytes=VMEM_LIMIT),
        cost_estimate=COST,
        name="norm_rows",
    )(u, micro, stats, gain[None], shift[None])


def pool_kernel(u_ref, micro_ref, stats_ref, *refs):
    parts, (total_ref, pooled_ref) = refs[:-2], refs[-2:]
    stats = stats_ref[...]
    scale = lax.rsqrt(stats[2 * MB :] / stats[:MB] + EPSILON)
    micro = micro_ref[...]
    standard = (u_ref[...].astype(F32) - pick(micro, stats[MB : 2 * MB])) * pick(micro, scale)
    total = sum(ref[...] for ref in parts)
    total_ref[...] = total
    product = total * standard
    for b in range(MB):
        pooled_ref[b : b + 1, :] = jnp.sum(jnp.where(micro == b, total, 0.0), axis=0, keepdims=True)
        pooled_ref[MB + b : MB + b + 1, :] = jnp.sum(jnp.where(micro == b, product, 0.0), axis=0, keepdims=True)


def pool_grads(u, micro, stats, parts):
    rows, cols = u.shape
    return pl.pallas_call(
        pool_kernel,
        out_shape=[jax.ShapeDtypeStruct((rows, cols), F32), jax.ShapeDtypeStruct((2 * MB, cols), F32)],
        compiler_params=pltpu.CompilerParams(vmem_limit_bytes=VMEM_LIMIT),
        cost_estimate=COST,
        name="pool_grads",
    )(u, micro, stats, *parts)


def carry_kernel(u_ref, micro_ref, valid_ref, stats_ref, gain_ref, total_ref, pooled_ref, carried_ref, out_ref):
    stats = stats_ref[...]
    gain = gain_ref[...]
    counts = stats[:MB]
    scale = lax.rsqrt(stats[2 * MB :] / counts + EPSILON)
    pooled = pooled_ref[...]
    micro = micro_ref[...]
    row_scale = pick(micro, scale)
    standard = (u_ref[...].astype(F32) - pick(micro, stats[MB : 2 * MB])) * row_scale
    shift_term = pick(micro, gain * pooled[:MB] / counts)
    scale_term = pick(micro, gain * pooled[MB:] / counts)
    out_ref[...] = carried_ref[...] + row_scale * (
        total_ref[...] * gain - valid_ref[...] * (shift_term + standard * scale_term)
    )


def carry_grads(u, micro, valid, stats, gain, total, pooled, carried):
    rows, cols = u.shape
    return pl.pallas_call(
        carry_kernel,
        out_shape=jax.ShapeDtypeStruct((rows, cols), F32),
        compiler_params=pltpu.CompilerParams(vmem_limit_bytes=VMEM_LIMIT),
        cost_estimate=COST,
        name="carry_grads",
    )(u, micro, valid, stats, gain[None], total, pooled, carried)


def feature_mask(logits, thresh):
    centred = logits - jnp.max(logits)
    weights = jnp.exp(centred) * jax.nn.softplus(centred + thresh)
    return weights / jnp.sum(weights)


def combine_kernel(plan, n_in, n_tokens, *refs):
    ins, outs = refs[:n_in], refs[n_in + n_tokens :]
    for out, slots in zip(outs, plan):
        for s, terms in enumerate(slots):
            if len(terms) == 1:
                out[s, 0] = ins[terms[0][0]][terms[0][1], 0]
            else:
                out[s, 0] = sum(ins[k][j, 0].astype(F32) for k, j in terms).astype(out.dtype)


def combine(plan, parts, tokens=()):
    parts = [p if isinstance(p, tuple) else (p, p.shape[0], 0) for p in parts]
    out_n = [{p[0].shape[1] for p, used in zip(parts, uses) if used} for uses in uses_of(plan, len(parts))]
    pr, width = parts[0][0].shape[2:]
    n = max(max(v) for v in out_n)
    step = pr

    def block(slots, at, size):
        if size == n:
            return pl.BlockSpec((slots, 1, step, width), lambda i, r: (at, i, r, 0))
        return pl.BlockSpec((slots, 1, step, width), lambda i, r: (at, jnp.minimum(i, size - 1), r, 0))

    return pl.pallas_call(
        functools.partial(combine_kernel, plan, len(parts), len(tokens)),
        grid=(n, pr // step),
        in_specs=[block(slots, at, a.shape[1]) for a, slots, at in parts]
        + [pl.BlockSpec(memory_space=pl.ANY)] * len(tokens),
        out_specs=[block(len(slots), 0, min(v)) for slots, v in zip(plan, out_n)],
        out_shape=[jax.ShapeDtypeStruct((len(slots), min(v), pr, width), BF16) for slots, v in zip(plan, out_n)],
        compiler_params=pltpu.CompilerParams(vmem_limit_bytes=VMEM_LIMIT),
        cost_estimate=LONG,
        name="combine",
    )(*[p[0] for p in parts], *tokens)


def uses_of(plan, n_parts):
    return [[any(k == part for terms in slots for k, _ in terms) for part in range(n_parts)] for slots in plan]


def pack_kernel(place, g_in, g_out, *refs):
    out = refs[-1]
    wide = g_in.shape[-1]
    out[0, 0, :, :wide] = g_in[0]
    out[0, 0, :, wide:] = g_out[0]


def pack(place, gate_in, gate_out, lo, hi, rows, tokens):
    wide, cols = gate_in.shape[-1], gate_out.shape[-1]
    block = lambda w: pl.BlockSpec((1, rows, w), lambda i, place: (lo + i, place[0], 0))
    return pl.pallas_call(
        pack_kernel,
        grid_spec=pltpu.PrefetchScalarGridSpec(
            num_scalar_prefetch=1,
            grid=(hi - lo,),
            in_specs=[block(wide), block(cols)] + [pl.BlockSpec(memory_space=pl.ANY)] * len(tokens),
            out_specs=pl.BlockSpec((1, 1, rows, wide + cols), lambda i, place: (0, i, 0, 0)),
        ),
        out_shape=jax.ShapeDtypeStruct((1, hi - lo, rows, wide + cols), BF16),
        cost_estimate=COST,
        name="pack",
    )(place, gate_in, gate_out, *tokens)


def along(axis, size, flip):
    return [(i, i ^ flip) for i in range(size)]


def tie_kernel(*refs):
    pass


def tie(arrays, tokens):
    if not tokens:
        return list(arrays)
    any_spec = pl.BlockSpec(memory_space=pl.ANY)
    return pl.pallas_call(
        tie_kernel,
        in_specs=[any_spec] * (len(arrays) + len(tokens)),
        out_specs=[any_spec] * len(arrays),
        out_shape=[jax.ShapeDtypeStruct(a.shape, a.dtype) for a in arrays],
        input_output_aliases={i: i for i in range(len(arrays))},
        cost_estimate=COST,
        name="tie",
    )(*arrays, *tokens)


def low_sum(*terms):
    return sum(v.astype(F32) for v in terms).astype(BF16)


class CubeTransfers:
    def __init__(self, dp_size, fsdp_size):
        self.dp_size, self.fsdp_size = dp_size, fsdp_size
        self.slots = [4, 4, 4, 2, 2, 16]
        self.ring_slots = [dp_size * fsdp_size // 2] * 2

    def core(self, v):
        return lax.ppermute(v, "dp", along("dp", self.dp_size, 1))

    def x(self, v):
        return lax.ppermute(v, "dp", along("dp", self.dp_size, 2))

    def y(self, v):
        return lax.ppermute(v, "fsdp", along("fsdp", self.fsdp_size, 1))

    def z(self, v, flip):
        return lax.ppermute(v, "fsdp", along("fsdp", self.fsdp_size, 2 * flip))

    def far(self, v):
        size = self.dp_size * self.fsdp_size
        return lax.ppermute(v, ("dp", "fsdp"), along(("dp", "fsdp"), size, 2 * self.fsdp_size + 1))

    def all_reduce(self, v, merge):
        v = merge(v, self.core(v))
        v = merge(merge(v, self.x(v)), merge(self.y(v), self.far(v)))
        return merge(merge(v, self.z(v, 1)), merge(self.z(v, 2), self.z(v, 3)))

    def table(self, shard_rows):
        q = lax.axis_index("dp").astype(jnp.int32)
        f = lax.axis_index("fsdp").astype(jnp.int32)
        rows = []
        for core in (0, 1):
            for flip_q, flip_y, slots in ((0, 0, range(4)), (0, 1, range(4)), (2, 0, range(4)), (2, 1, range(4))):
                for j in slots:
                    place = f ^ (2 * j + flip_y)
                    rows.append(place * shard_rows + (q ^ (flip_q + core)) * (shard_rows // self.dp_size))
        return jnp.stack(rows)


    def ring_table(self, shard_rows):
        rows = shard_rows // self.dp_size
        core = lax.axis_index("dp").astype(jnp.int32) % 2
        order = [(f, x) for x in range(self.dp_size // 2) for f in range(self.fsdp_size)]
        halves = [jnp.array([f * shard_rows + 2 * x * rows for f, x in order], jnp.int32) + c * rows for c in (core, 1 - core)]
        return jnp.concatenate(halves)

    def ring_core(self, parts):
        return parts[0], self.core(parts[1])

    def ring_sums(self, parts):
        halves = jnp.concatenate([low_sum(*part) for part in parts], axis=1)
        same = [[d * self.fsdp_size + f for d in range(c, self.dp_size, 2) for f in range(self.fsdp_size)] for c in (0, 1)]
        own = lax.psum_scatter(halves, ("dp", "fsdp"), scatter_dimension=0, axis_index_groups=same)[None]
        return self.dp_pieces(own)
        yield


    def begin(self, gate_in, gate_out, lo, hi, tokens=()):
        place = lax.axis_index("dp").astype(jnp.int32)[None]
        own = pack(place, gate_in, gate_out, lo, hi, gate_in.shape[1] // self.dp_size, tokens)
        return [own] + [self.z(own, j) for j in (1, 2, 3)]

    def spread(self, pieces, tokens=()):
        (held,) = combine([[[(k, 0)] for k in range(4)]], pieces, tokens)
        return held, self.y(held), self.x(held)

    def relay(self, arrays, tokens=()):
        held, by_y, by_x = arrays
        half_y, half_x = combine([[[(0, 0)], [(0, 1)]], [[(1, 0)], [(1, 1)]]], [(by_y, 2, 0), (by_x, 2, 1)], tokens)
        return [held, by_y, by_x, self.x(half_y), self.y(half_x)], half_y

    def finish(self, mine):
        return mine + [self.core(v) for v in mine]


    def sums(self, parts):
        held, by_y, by_x, far_x, far_y, other = parts
        other = self.core(other)
        far_x, far_y = yield [low_sum(far_x, other[12:14]), low_sum(far_y, other[14:16])]
        got_x, got_y = self.x(far_x), self.y(far_y)
        by_y = jnp.concatenate([low_sum(by_y[:2], other[4:6], got_x), low_sum(by_y[2:], other[6:8])])
        by_x = jnp.concatenate([low_sum(by_x[:2], other[8:10]), low_sum(by_x[2:], other[10:12], got_y)])
        by_y, by_x = yield [by_y, by_x]
        got_y, got_x = self.y(by_y), self.x(by_x)
        held = [low_sum(*(v[k : k + 1] for v in (held, other, got_y, got_x))) for k in range(4)]
        sent = yield held[1:]
        own = low_sum(held[0], *(self.z(v, k + 1) for k, v in enumerate(sent)))
        (own,) = yield [own]
        return self.dp_pieces(own)

    def dp_pieces(self, own):
        by_x = self.x(own)
        return [own, self.core(own), by_x, self.core(by_x)]

    def pieces_table(self, shard_rows):
        q = lax.axis_index("dp").astype(jnp.int32)
        return jnp.stack([(q ^ j) * (shard_rows // self.dp_size) for j in range(4)])


class PlainTransfers:
    def __init__(self, dp_size, fsdp_size):
        self.fsdp_size = fsdp_size
        self.slots = self.ring_slots = [fsdp_size]

    def all_reduce(self, v, merge):
        every = lax.all_gather(v, ("dp", "fsdp"))
        while every.shape[0] > 1:
            half = every.shape[0] // 2
            every = jax.vmap(merge)(every[:half], every[half:])
        return every[0]

    def table(self, shard_rows):
        return jnp.arange(self.fsdp_size, dtype=jnp.int32) * shard_rows

    ring_table = table

    def ring_core(self, parts):
        return parts

    def begin(self, gate_in, gate_out, lo, hi, tokens=()):
        return jnp.concatenate([gate_in[lo:hi], gate_out[lo:hi]], axis=-1)

    def spread(self, shard, tokens=()):
        return [lax.all_gather(shard, "fsdp")]

    def relay(self, arrays, tokens=()):
        return arrays, arrays[0]

    def finish(self, mine):
        return mine

    def sums(self, parts):
        own = lax.psum_scatter(parts[0], "fsdp", scatter_dimension=0)
        return [lax.psum(own, "dp")[None]]
        yield

    def ring_sums(self, parts):
        return (yield from self.sums([jnp.concatenate([part[0] for part in parts], axis=1)]))

    def pieces_table(self, shard_rows):
        return jnp.zeros((1,), jnp.int32)


def place_kernel(n_pieces, table, *refs):
    pieces = refs[:n_pieces]
    g_in, g_out = refs[-2:]
    pr = pieces[0].shape[2]
    wide = g_in.shape[-1]
    for j, piece in enumerate(pieces):
        row = pl.multiple_of(table[j], pr)
        value = piece[0, 0].astype(F32)
        g_in[0, pl.ds(row, pr), :] = value[:, :wide]
        g_out[0, pl.ds(row, pr), :] = value[:, wide:]


def place_grads(table, pieces, start, shard_rows, previous):
    _, n, pr, width = pieces[0].shape
    wide = 2 * width // 3
    shapes = [
        jax.ShapeDtypeStruct((LAYERS * SECTIONS, shard_rows, wide), F32),
        jax.ShapeDtypeStruct((LAYERS * SECTIONS, shard_rows, width - wide), F32),
    ]
    block = lambda w: pl.BlockSpec((1, shard_rows, w), lambda i, *_: (start + i, 0, 0))
    n_pieces = len(pieces)
    extra = [] if previous is None else list(previous)
    return pl.pallas_call(
        functools.partial(place_kernel, n_pieces),
        grid_spec=pltpu.PrefetchScalarGridSpec(
            num_scalar_prefetch=1,
            grid=(n,),
            in_specs=[pl.BlockSpec((1, 1, pr, width), lambda i, *_: (0, i, 0, 0))] * n_pieces
            + [pl.BlockSpec(memory_space=pl.ANY)] * len(extra),
            out_specs=[block(wide), block(width - wide)],
        ),
        out_shape=shapes,
        input_output_aliases={} if previous is None else {1 + n_pieces: 0, 2 + n_pieces: 1},
        cost_estimate=COST,
        name="place_grads",
    )(table, *pieces, *extra)


def local(
    moves,
    features,
    row_valid,
    micro_batch,
    gains,
    shifts,
    mask_logits,
    thresholds,
    gate_in,
    bias_in,
    gate_out,
    bias_out,
    cotangent,
):
    columns = features.shape[1]
    shard_rows = gate_in.shape[2]
    valid = row_valid.astype(F32)[:, None]
    micro = micro_batch[:, None]
    tables = (moves.table(shard_rows), moves.ring_table(shard_rows))
    flat = lambda v: v.reshape((LAYERS * SECTIONS,) + v.shape[2:])
    gate_in, gate_out, bias_in, bias_out = flat(gate_in), flat(gate_out), flat(bias_in), flat(bias_out)
    masks = columns * flat(jax.vmap(jax.vmap(feature_mask))(mask_logits, thresholds))
    add = lambda a, b: a + b
    begin = lambda j, tokens=(): moves.begin(gate_in, gate_out, *GATHERS[j], tokens)

    gathered, records, stored = [], [], []
    current, hidden = features, None
    _, stats = local_stats(current, None, micro, valid)
    begun = {0: begin(0)}
    spreads = {0: moves.spread(begun[0], (stats,))}
    begun[1] = begin(1, (spreads[0][0],))
    stats = moves.all_reduce(stats, merge_stats)
    before = ()
    for k, (lo, hi) in enumerate(GATHERS):
        layer = lo // SECTIONS
        if lo % SECTIONS == 0:
            if k > 0:
                current, stats = local_stats(current, hidden, micro, valid)
                stats = moves.all_reduce(stats, merge_stats)
                before = (stats,)
            normed, x_turned = norm_rows(current, micro, stats, gains[layer], shifts[layer])
            hidden = normed
            records.append((current, stats, normed, x_turned))
        arrays, token = moves.relay(spreads[k], before)
        tokens = [token]
        if k + 1 < len(GATHERS):
            spreads[k + 1] = moves.spread(begun[k + 1], tokens)
            tokens = [spreads[k + 1][0]]
        if k + 2 < len(GATHERS):
            begun[k + 2] = begin(k + 2, tokens)
            tokens = [begun[k + 2][0]]
        arrays = moves.finish(arrays)
        hidden, *saved = forward_chunk(
            tables[0], hidden, normed, masks[lo:hi], bias_in[lo:hi], bias_out[lo:hi], arrays, 0, tokens
        )
        before = (hidden,)
        stored.append((lo, hi, arrays, saved))
    mixed_out = (current + hidden).astype(BF16)

    carried = cotangent.astype(F32) * valid
    pieces_table = moves.pieces_table(shard_rows)
    grads = None
    results = [None] * LAYERS
    under_way = []
    tokens = []

    def advance(item, sent):
        try:
            item[1] = item[0].send(sent)
            return True
        except StopIteration as stop:
            item[2](stop.value)
            return False

    def start(generator, at_end):
        item = [generator, None, at_end]
        if advance(item, None):
            under_way.append(item)

    def send_all(after=None):
        ready = [item[1] for item in under_way]
        if after is not None:
            tied = iter(tie([v for sent in ready for v in sent], after))
            ready = [[next(tied) for _ in sent] for sent in ready]
        made = [v for sent in ready for v in sent]
        under_way[:] = [item for item, sent in zip(list(under_way), ready) if advance(item, sent)]
        return made

    def placed(lo):
        def at_end(pieces):
            nonlocal grads
            grads = place_grads(pieces_table, pieces, lo, shard_rows, grads)

        return at_end

    ring_parts = []
    for k, (lo, hi) in reversed(list(enumerate(GROUPS))):
        layer = lo // SECTIONS
        current, stats, normed, x_turned = records[layer]
        if hi % SECTIONS == 0:
            gh = carried
            normed_parts, vectors = [], []
        ((start_at, _, arrays, saved),) = [g for g in stored if g[0] <= lo and hi <= g[1]]
        ring = RING_SUM[0] <= lo < RING_SUM[1]
        gh, gn, g_mask, g_bin, g_bout, out = backward_chunk(
            jnp.concatenate([tables[0], tables[1 if ring else 0]]),
            gh,
            normed,
            x_turned,
            masks[lo:hi],
            saved,
            lo - start_at,
            arrays,
            lo - start_at,
            moves.ring_slots if ring else moves.slots,
            tokens,
        )
        normed_parts.append(gn)
        vectors.insert(0, jnp.concatenate([g_mask, g_bin, g_bout], axis=1))
        tokens = []
        if ring:
            ring_parts.insert(0, moves.ring_core(out))
        else:
            start(moves.sums(out), placed(lo))
            if k > 0:
                tokens = send_all()
        if lo % SECTIONS == 0:
            total, pooled = pool_grads(current, micro, stats, normed_parts + [gh])
            vectors = jnp.concatenate(vectors, axis=0)
            results[layer] = moves.all_reduce(jnp.concatenate([pooled, vectors.reshape(-1, columns)]), add)
            carried = carry_grads(current, micro, valid, stats, gains[layer], total, results[layer][: 2 * MB], carried)
    after = [carried]
    while under_way:
        after = send_all(after) + list(grads or ())
    start(moves.ring_sums(ring_parts), placed(RING_SUM[0]))
    pooled = jnp.stack([both[: 2 * MB] for both in results])
    stacked = jnp.stack([both[2 * MB :].reshape(SECTIONS, 4 * columns) for both in results])
    _, mask_pull = jax.vjp(jax.vmap(jax.vmap(feature_mask)), mask_logits, thresholds)
    grad_logits, grad_thresholds = mask_pull(stacked[..., :columns])
    unflat = lambda v: v.reshape((LAYERS, SECTIONS) + v.shape[1:])
    return (
        mixed_out,
        carried,
        jnp.sum(pooled[:, MB:], axis=1),
        jnp.sum(pooled[:, :MB], axis=1),
        grad_logits,
        grad_thresholds,
        unflat(grads[0]),
        stacked[..., columns : 3 * columns],
        unflat(grads[1]),
        stacked[..., 3 * columns :],
    )


def solution(mesh):
    rows = P(("dp", "fsdp"), None)
    row = P(("dp", "fsdp"))
    shard = P(None, None, "fsdp", None)
    in_specs = (rows, row, row, P(), P(), P(), P(), shard, P(), shard, P(), rows)
    out_specs = (rows, rows, P(), P(), P(), P(), shard, P(), shard, P())
    dp_size, fsdp_size = mesh.shape["dp"], mesh.shape["fsdp"]
    kind = CubeTransfers if (dp_size, fsdp_size) == (4, 8) else PlainTransfers
    return jax.shard_map(
        functools.partial(local, kind(dp_size, fsdp_size)),
        mesh=mesh,
        in_specs=in_specs,
        out_specs=out_specs,
        check_vma=False,
    )
```

```python
import functools

import jax
import jax.numpy as jnp
from jax import lax
from jax.experimental import pallas as pl
from jax.experimental.pallas import tpu as pltpu
from jax.sharding import PartitionSpec as P

SECTIONS = 6
LAYERS = 2
MB = 4
BF16 = jnp.bfloat16
F32 = jnp.float32
EPSILON = 1e-05
TILE = 256
COST = pl.CostEstimate(flops=1, bytes_accessed=1, transcendentals=0)
LONG = pl.CostEstimate(flops=2 * 10**10, bytes_accessed=1, transcendentals=0)
VMEM_LIMIT = 60 * 1024 * 1024
GATHERS = ((0, 3), (3, 6), (6, 12))
GROUPS = ((0, 3), (3, 6), (6, 9), (9, 12))


def gate(x):
    return 0.5 * jnp.tanh(0.5 * x) + 0.5


def load_weights(table, arrays, wbuf, sems, n, pr, first):
    for part, lo, hi in ((0, 0, 1), (1, 1, n)):
        if lo == hi:
            continue
        at = 0
        for array in arrays:
            for slot in range(array.shape[0]):
                row = pl.multiple_of(table[at], pr)
                pltpu.make_async_copy(
                    array.at[slot, pl.ds(first + lo, hi - lo)],
                    wbuf.at[pl.ds(lo, hi - lo), pl.ds(row, pr)],
                    sems.at[part],
                ).start()
                at += 1


def wait_weights(wbuf, sems, n, part):
    lo, hi = (0, 1) if part == 0 else (1, n)
    whole = wbuf.at[pl.ds(lo, hi - lo)]
    pltpu.make_async_copy(whole, whole, sems.at[part]).wait()


def forward_kernel(n, first, n_arrays, n_tokens, final, pr, tile, table, *refs):
    base, refs = (refs[0], refs[1:]) if final else (None, refs)
    hidden_in, normed, mask, bias_in, bias_out = refs[:5]
    arrays = refs[5 : 5 + n_arrays]
    refs = refs[n_tokens:]
    hidden_out = refs[5 + n_arrays]
    factors = refs[6 + n_arrays : 11 + n_arrays]
    h_turned, rh_turned = refs[11 + n_arrays : 13 + n_arrays]
    wbuf, hid, sems = refs[13 + n_arrays :]
    step = pl.program_id(0)
    rows, cols = hid.shape

    @pl.when(step == 0)
    def _():
        load_weights(table, arrays, wbuf, sems, n, pr, first)
        hid[...] = hidden_in[...]
        wait_weights(wbuf, sems, n, 0)

    if n > 1:
        @pl.when(step == 1)
        def _():
            wait_weights(wbuf, sems, n, 1)

    w = wbuf.at[step]
    mask_row = mask[0]
    b_in = bias_in[0]
    b_out = bias_out[0]

    for t in range(rows // tile):
        at = slice(t * tile, (t + 1) * tile)
        h = hid[at, :]
        x = normed[at, :]
        low_h = h.astype(BF16)
        first_in = jnp.concatenate([(mask_row * x).astype(BF16), low_h], axis=1)
        pre = jnp.dot(first_in, w[:, : 2 * cols], preferred_element_type=F32) + b_in
        update = gate(pre[:, :cols])
        reset = gate(pre[:, cols:])
        low_rh = (reset * h).astype(BF16)
        second_in = jnp.concatenate([low_rh, x.astype(BF16)], axis=1)
        raw = jnp.dot(second_in, w[:, 2 * cols :], preferred_element_type=F32) + b_out
        cand = jnp.tanh(raw)
        keep = 1.0 - update
        apart = cand - h
        hid[at, :] = h + update * apart
        values = (update * (1.0 - cand * cand), apart * update * keep, h * reset * (1.0 - reset), keep, reset)
        for ref, value in zip(factors, values):
            ref[0, at, :] = value.astype(ref.dtype)
        h_turned[0, :, at] = low_h.T
        rh_turned[0, :, at] = low_rh.T

    @pl.when(step == n - 1)
    def _():
        hidden_out[...] = (base[...] + hid[...]).astype(BF16) if final else hid[...]


def forward_chunk(table, lo, hi, hidden, normed, masks, bias_in, bias_out, arrays, first, tokens=(), base=None, tile=TILE):
    n = hi - lo
    bases = () if base is None else (base,)
    rows, cols = hidden.shape
    pr = arrays[0].shape[2]
    depth = 2 * cols
    whole = pl.BlockSpec((rows, cols), lambda i, *_: (0, 0))
    row = lambda width: pl.BlockSpec((1, 1, width), lambda i, *_: (lo + i, 0, 0))
    per = pl.BlockSpec((1, rows, cols), lambda i, *_: (i, 0, 0))
    turned = pl.BlockSpec((1, cols, rows), lambda i, *_: (i, 0, 0))
    saved = [jax.ShapeDtypeStruct((n, rows, cols), t) for t in (F32,) * 5] + [jax.ShapeDtypeStruct((n, cols, rows), BF16)] * 2
    return pl.pallas_call(
        functools.partial(forward_kernel, n, first, len(arrays), len(tokens), base is not None, pr, tile),
        grid_spec=pltpu.PrefetchScalarGridSpec(
            num_scalar_prefetch=1,
            grid=(n,),
            in_specs=[whole] * len(bases) + [whole, whole, row(cols), row(2 * cols), row(cols)]
            + [pl.BlockSpec(memory_space=pl.ANY)] * (len(arrays) + len(tokens)),
            out_specs=[whole] + [per] * 5 + [turned] * 2,
            scratch_shapes=[
                pltpu.VMEM((n, depth, 3 * cols), BF16),
                pltpu.VMEM((rows, cols), F32),
                pltpu.SemaphoreType.DMA((2,)),
            ],
        ),
        out_shape=[jax.ShapeDtypeStruct((rows, cols), F32 if base is None else BF16)] + saved,
        compiler_params=pltpu.CompilerParams(vmem_limit_bytes=VMEM_LIMIT),
        cost_estimate=LONG,
        name="forward_sections",
    )(table, *bases, hidden, normed, masks, bias_in, bias_out, *arrays, *tokens)


def backward_kernel(n, first, n_in, n_out, n_tokens, pr, tile, table, *refs):
    gh_in, normed, x_turned, mask = refs[:4]
    factors = refs[4:9]
    h_turned, rh_turned = refs[9:11]
    arrays = refs[11 : 11 + n_in]
    refs = refs[11 + n_in + n_tokens :]
    gh_out, gn_out, vectors = refs[:3]
    outs = refs[3 : 3 + n_out]
    wbuf, gh, gn, gg, gr, stage, sems, out_sems = refs[3 + n_out :]
    step = pl.program_id(0)
    sec = n - 1 - step
    rows, cols = gh.shape
    wide = 2 * cols

    def wait_out(slot):
        whole = stage.at[slot]
        pltpu.make_async_copy(whole, whole, out_sems.at[slot]).wait()

    @pl.when(step == 0)
    def _():
        for part, lo, hi in ((0, n - 1, n), (1, 0, n - 1)):
            if lo == hi:
                continue
            at = 0
            for array in arrays:
                for slot in range(array.shape[0]):
                    row = pl.multiple_of(table[at], pr)
                    pltpu.make_async_copy(
                        array.at[slot, pl.ds(first + lo, hi - lo)],
                        wbuf.at[pl.ds(lo, hi - lo), pl.ds(row, pr)],
                        sems.at[part],
                    ).start()
                    at += 1
        gh[...] = gh_in[...]
        gn[...] = jnp.zeros_like(gn)
        whole = wbuf.at[pl.ds(n - 1, 1)]
        pltpu.make_async_copy(whole, whole, sems.at[0]).wait()

    if n > 1:
        @pl.when(step == 1)
        def _():
            whole = wbuf.at[pl.ds(0, n - 1)]
            pltpu.make_async_copy(whole, whole, sems.at[1]).wait()

    w = wbuf.at[sec]
    mask_row = mask[0]
    nt = (((1,), (1,)), ((), ()))

    m_sum = jnp.zeros((1, cols), F32)
    bi_sum = jnp.zeros((1, wide), F32)
    bo_sum = jnp.zeros((1, cols), F32)
    for t in range(rows // tile):
        at = slice(t * tile, (t + 1) * tile)
        g = gh[at, :]
        by_raw, by_update, by_reset, keep, reset = (ref[0, at, :].astype(F32) for ref in factors)
        grad_raw = (g * by_raw).astype(BF16)
        gr[at, :] = grad_raw
        second = lax.dot_general(grad_raw, w[:, wide:], nt, preferred_element_type=F32)
        g2 = second[:, :cols]
        gates = jnp.concatenate([(g * by_update).astype(BF16), (g2 * by_reset).astype(BF16)], axis=1)
        gg[at, :] = gates
        first = lax.dot_general(gates, w[:, :wide], nt, preferred_element_type=F32)
        gm = first[:, :cols]
        gn[at, :] = gn[at, :] + second[:, cols:] + gm * mask_row
        gh[at, :] = g * keep + g2 * reset + first[:, cols:]
        m_sum = m_sum + jnp.sum(gm * normed[at, :], axis=0, keepdims=True)
        bi_sum = bi_sum + jnp.sum(gates.astype(F32), axis=0, keepdims=True)
        bo_sum = bo_sum + jnp.sum(grad_raw.astype(F32), axis=0, keepdims=True)
    vectors[0, :, :cols] = m_sum * float(cols)
    vectors[0, :, cols : 3 * cols] = bi_sum
    vectors[0, :, 3 * cols :] = bo_sum

    slot = lax.rem(step, 2)
    if n > 2:
        @pl.when(step >= 2)
        def _():
            wait_out(slot)

    stage[slot, :cols, wide:] = jnp.dot(rh_turned[0], gr[...], preferred_element_type=F32).astype(BF16)
    stage[slot, cols:, wide:] = jnp.dot(x_turned[...], gr[...], preferred_element_type=F32).astype(BF16)
    masked = jnp.dot(x_turned[...], gg[...], preferred_element_type=F32)
    mask_column = jnp.broadcast_to(mask_row, (128, cols)).T[:, :1]
    stage[slot, :cols, :wide] = (masked * mask_column).astype(BF16)
    stage[slot, cols:, :wide] = jnp.dot(h_turned[0], gg[...], preferred_element_type=F32).astype(BF16)

    at = sum(array.shape[0] for array in arrays)
    for out in outs:
        for s in range(out.shape[0]):
            row = pl.multiple_of(table[at], pr)
            pltpu.make_async_copy(stage.at[slot, pl.ds(row, pr)], out.at[s, sec], out_sems.at[slot]).start()
            at += 1

    @pl.when(step == n - 1)
    def _():
        gh_out[...] = gh[...]
        gn_out[...] = gn[...]
        if n > 1:
            wait_out(1 - slot)
        wait_out(slot)


def backward_chunk(table, lo, hi, gh, normed, x_turned, masks, saved, arrays, first, out_slots, tokens=(), tile=TILE):
    n = hi - lo
    rows, cols = gh.shape
    pr = arrays[0].shape[2]
    depth = 2 * cols
    whole = pl.BlockSpec((rows, cols), lambda i, *_: (0, 0))
    row = lambda width: pl.BlockSpec((1, 1, width), lambda i, *_: (hi - 1 - i, 0, 0))
    turned = pl.BlockSpec((1, cols, rows), lambda i, *_: (first + n - 1 - i, 0, 0))
    per = pl.BlockSpec((1, rows, cols), lambda i, *_: (first + n - 1 - i, 0, 0))
    any_spec = pl.BlockSpec(memory_space=pl.ANY)
    state = jax.ShapeDtypeStruct((rows, cols), F32)
    results = pl.pallas_call(
        functools.partial(backward_kernel, n, first, len(arrays), len(out_slots), len(tokens), pr, tile),
        grid_spec=pltpu.PrefetchScalarGridSpec(
            num_scalar_prefetch=1,
            grid=(n,),
            in_specs=[whole, whole, pl.BlockSpec((cols, rows), lambda i, *_: (0, 0)), row(cols)]
            + [per] * 5
            + [turned] * 2
            + [any_spec] * (len(arrays) + len(tokens)),
            out_specs=[whole, whole, pl.BlockSpec((1, 1, 2 * depth), lambda i, *_: (n - 1 - i, 0, 0))] + [any_spec] * len(out_slots),
            scratch_shapes=[
                pltpu.VMEM((n, depth, 3 * cols), BF16),
                pltpu.VMEM((rows, cols), F32),
                pltpu.VMEM((rows, cols), F32),
                pltpu.VMEM((rows, depth), BF16),
                pltpu.VMEM((rows, cols), BF16),
                pltpu.VMEM((2, depth, 3 * cols), BF16),
                pltpu.SemaphoreType.DMA((2,)),
                pltpu.SemaphoreType.DMA((2,)),
            ],
        ),
        out_shape=[state, state, jax.ShapeDtypeStruct((n, 1, 2 * depth), F32)]
        + [jax.ShapeDtypeStruct((s, n, pr, 3 * cols), BF16) for s in out_slots],
        compiler_params=pltpu.CompilerParams(vmem_limit_bytes=VMEM_LIMIT),
        cost_estimate=LONG,
        name="backward_sections",
    )(table, gh, normed, x_turned, masks, *saved, *arrays, *tokens)
    return *results[:3], results[3:]


def pick(micro, table):
    out = table[MB - 1 : MB, :]
    for b in range(MB - 2, -1, -1):
        out = jnp.where(micro == b, table[b : b + 1, :], out)
    return out


def stats_kernel(with_hidden, n_tokens, *refs):
    if with_hidden:
        refs = refs[:4] + refs[4 + n_tokens :]
        u_ref, hidden_ref, micro_ref, valid_ref, out_ref, stats_ref = refs
        u = u_ref[...] + hidden_ref[...]
        out_ref[...] = u
    else:
        u_ref, micro_ref, valid_ref, stats_ref = refs
        u = u_ref[...].astype(F32)
    micro = micro_ref[...]
    valid = valid_ref[...]
    width = u.shape[1]
    counts, means = [], []
    for b in range(MB):
        member = jnp.where(micro == b, valid, 0.0)
        count = jnp.sum(member)
        total = jnp.sum(u * member, axis=0, keepdims=True)
        counts.append(jnp.full((1, width), count, F32))
        means.append(total / jnp.maximum(count, 1.0))
    centred = u - pick(micro, jnp.concatenate(means, axis=0))
    squares = centred * centred * valid
    for b in range(MB):
        stats_ref[b : b + 1, :] = counts[b]
        stats_ref[MB + b : MB + b + 1, :] = means[b]
        stats_ref[2 * MB + b : 2 * MB + b + 1, :] = jnp.sum(jnp.where(micro == b, squares, 0.0), axis=0, keepdims=True)


def local_stats(u, hidden, micro, valid, tokens=()):
    rows, cols = u.shape
    stats = jax.ShapeDtypeStruct((3 * MB, cols), F32)
    args = (u, micro, valid) if hidden is None else (u, hidden, micro, valid)
    out = [stats] if hidden is None else [jax.ShapeDtypeStruct((rows, cols), F32), stats]
    res = pl.pallas_call(
        functools.partial(stats_kernel, hidden is not None, len(tokens)),
        in_specs=[pl.BlockSpec(memory_space=pltpu.VMEM)] * len(args) + [pl.BlockSpec(memory_space=pl.ANY)] * len(tokens),
        out_shape=out,
        compiler_params=pltpu.CompilerParams(vmem_limit_bytes=VMEM_LIMIT),
        cost_estimate=COST,
        name="local_stats",
    )(*args, *tokens)
    return (None, res[0]) if hidden is None else res


def merge_stats(a, b):
    na, ma, qa = a[:MB], a[MB : 2 * MB], a[2 * MB :]
    nb, mb, qb = b[:MB], b[MB : 2 * MB], b[2 * MB :]
    n = na + nb
    inverse = 1.0 / jnp.maximum(n, 1.0)
    apart = ma - mb
    return jnp.concatenate([n, (na * ma + nb * mb) * inverse, qa + qb + apart * apart * (na * nb * inverse)], axis=0)


def norm_kernel(u_ref, micro_ref, stats_ref, gain_ref, shift_ref, normed_ref, turned_ref):
    stats = stats_ref[...]
    scale = lax.rsqrt(stats[2 * MB :] / stats[:MB] + EPSILON)
    micro = micro_ref[...]
    standard = (u_ref[...].astype(F32) - pick(micro, stats[MB : 2 * MB])) * pick(micro, scale)
    normed = standard * gain_ref[...] + shift_ref[...]
    normed_ref[...] = normed
    turned_ref[...] = normed.astype(BF16).T


def norm_rows(u, micro, stats, gain, shift):
    rows, cols = u.shape
    return pl.pallas_call(
        norm_kernel,
        out_shape=[jax.ShapeDtypeStruct((rows, cols), F32), jax.ShapeDtypeStruct((cols, rows), BF16)],
        compiler_params=pltpu.CompilerParams(vmem_limit_bytes=VMEM_LIMIT),
        cost_estimate=COST,
        name="norm_rows",
    )(u, micro, stats, gain[None], shift[None])


def pool_kernel(n_parts, u_ref, micro_ref, stats_ref, *refs):
    parts, (total_ref, pooled_ref) = refs[:n_parts], refs[-2:]
    stats = stats_ref[...]
    scale = lax.rsqrt(stats[2 * MB :] / stats[:MB] + EPSILON)
    micro = micro_ref[...]
    standard = (u_ref[...].astype(F32) - pick(micro, stats[MB : 2 * MB])) * pick(micro, scale)
    total = sum(ref[...] for ref in parts)
    total_ref[...] = total
    product = total * standard
    for b in range(MB):
        pooled_ref[b : b + 1, :] = jnp.sum(jnp.where(micro == b, total, 0.0), axis=0, keepdims=True)
        pooled_ref[MB + b : MB + b + 1, :] = jnp.sum(jnp.where(micro == b, product, 0.0), axis=0, keepdims=True)


def in_vmem(arrays, tokens):
    vmem, any_spec = pl.BlockSpec(memory_space=pltpu.VMEM), pl.BlockSpec(memory_space=pl.ANY)
    return [vmem] * len(arrays) + [any_spec] * len(tokens)


def pool_grads(u, micro, stats, parts, tokens=()):
    rows, cols = u.shape
    args = (u, micro, stats, *parts)
    return pl.pallas_call(
        functools.partial(pool_kernel, len(parts)),
        in_specs=in_vmem(args, tokens),
        out_shape=[jax.ShapeDtypeStruct((rows, cols), F32), jax.ShapeDtypeStruct((2 * MB, cols), F32)],
        compiler_params=pltpu.CompilerParams(vmem_limit_bytes=VMEM_LIMIT),
        cost_estimate=LONG,
        name="pool_grads",
    )(*args, *tokens)


def carry_kernel(u_ref, micro_ref, valid_ref, stats_ref, gain_ref, total_ref, pooled_ref, carried_ref, *refs):
    out_ref = refs[-1]
    stats = stats_ref[...]
    gain = gain_ref[...]
    counts = stats[:MB]
    scale = lax.rsqrt(stats[2 * MB :] / counts + EPSILON)
    pooled = pooled_ref[...]
    micro = micro_ref[...]
    row_scale = pick(micro, scale)
    standard = (u_ref[...].astype(F32) - pick(micro, stats[MB : 2 * MB])) * row_scale
    shift_term = pick(micro, gain * pooled[:MB] / counts)
    scale_term = pick(micro, gain * pooled[MB:] / counts)
    out_ref[...] = carried_ref[...] + row_scale * (
        total_ref[...] * gain - valid_ref[...] * (shift_term + standard * scale_term)
    )


def carry_grads(u, micro, valid, stats, gain, total, pooled, carried, tokens=()):
    rows, cols = u.shape
    args = (u, micro, valid, stats, gain[None], total, pooled, carried)
    return pl.pallas_call(
        carry_kernel,
        in_specs=in_vmem(args, tokens),
        out_shape=jax.ShapeDtypeStruct((rows, cols), F32),
        compiler_params=pltpu.CompilerParams(vmem_limit_bytes=VMEM_LIMIT),
        cost_estimate=COST,
        name="carry_grads",
    )(*args, *tokens)


def feature_mask(logits, thresh):
    centred = logits - jnp.max(logits)
    weights = jnp.exp(centred) * jax.nn.softplus(centred + thresh)
    return weights / jnp.sum(weights)


def combine_kernel(plan, n_in, n_tokens, *refs):
    ins, outs = refs[:n_in], refs[n_in + n_tokens :]
    for out, slots in zip(outs, plan):
        for s, terms in enumerate(slots):
            if len(terms) == 1:
                out[s, 0] = ins[terms[0][0]][terms[0][1], 0]
            else:
                out[s, 0] = sum(ins[k][j, 0].astype(F32) for k, j in terms).astype(out.dtype)


def combine(plan, parts, tokens=()):
    parts = [p if isinstance(p, tuple) else (p, p.shape[0], 0) for p in parts]
    out_n = [{p[0].shape[1] for p, used in zip(parts, uses) if used} for uses in uses_of(plan, len(parts))]
    pr, width = parts[0][0].shape[2:]
    n = max(max(v) for v in out_n)
    step = pr

    def block(slots, at, size):
        if size == n:
            return pl.BlockSpec((slots, 1, step, width), lambda i, r: (at, i, r, 0))
        return pl.BlockSpec((slots, 1, step, width), lambda i, r: (at, jnp.minimum(i, size - 1), r, 0))

    return pl.pallas_call(
        functools.partial(combine_kernel, plan, len(parts), len(tokens)),
        grid=(n, pr // step),
        in_specs=[block(slots, at, a.shape[1]) for a, slots, at in parts]
        + [pl.BlockSpec(memory_space=pl.ANY)] * len(tokens),
        out_specs=[block(len(slots), 0, min(v)) for slots, v in zip(plan, out_n)],
        out_shape=[jax.ShapeDtypeStruct((len(slots), min(v), pr, width), BF16) for slots, v in zip(plan, out_n)],
        compiler_params=pltpu.CompilerParams(vmem_limit_bytes=VMEM_LIMIT),
        cost_estimate=LONG,
        name="combine",
    )(*[p[0] for p in parts], *tokens)


def uses_of(plan, n_parts):
    return [[any(k == part for terms in slots for k, _ in terms) for part in range(n_parts)] for slots in plan]


def pack_kernel(place, g_in, g_out, *refs):
    out = refs[-1]
    wide = g_in.shape[-1]
    out[0, 0, :, :wide] = g_in[0]
    out[0, 0, :, wide:] = g_out[0]


def pack(place, gate_in, gate_out, lo, hi, rows, tokens):
    wide, cols = gate_in.shape[-1], gate_out.shape[-1]
    block = lambda w: pl.BlockSpec((1, rows, w), lambda i, place: (lo + i, place[0], 0))
    return pl.pallas_call(
        pack_kernel,
        grid_spec=pltpu.PrefetchScalarGridSpec(
            num_scalar_prefetch=1,
            grid=(hi - lo,),
            in_specs=[block(wide), block(cols)] + [pl.BlockSpec(memory_space=pl.ANY)] * len(tokens),
            out_specs=pl.BlockSpec((1, 1, rows, wide + cols), lambda i, place: (0, i, 0, 0)),
        ),
        out_shape=jax.ShapeDtypeStruct((1, hi - lo, rows, wide + cols), BF16),
        cost_estimate=COST,
        name="pack",
    )(place, gate_in, gate_out, *tokens)


def along(axis, size, flip):
    return [(i, i ^ flip) for i in range(size)]


def tie_kernel(*refs):
    pass


def tie(arrays, tokens):
    if not tokens:
        return list(arrays)
    any_spec = pl.BlockSpec(memory_space=pl.ANY)
    return pl.pallas_call(
        tie_kernel,
        in_specs=[any_spec] * (len(arrays) + len(tokens)),
        out_specs=[any_spec] * len(arrays),
        out_shape=[jax.ShapeDtypeStruct(a.shape, a.dtype) for a in arrays],
        input_output_aliases={i: i for i in range(len(arrays))},
        cost_estimate=COST,
        name="tie",
    )(*arrays, *tokens)


def low_sum(*terms):
    return sum(v.astype(F32) for v in terms).astype(BF16)


class Sending:
    def __init__(self, steps):
        self.steps, self.ready, self.result = steps, None, None
        self.resume(None)

    def resume(self, sent):
        try:
            self.ready = self.steps.send(sent)
        except StopIteration as stop:
            self.ready, self.result = None, stop.value

    def send(self, tokens):
        if self.ready is None:
            return list(tokens)
        sent = tie(self.ready, list(tokens))
        self.resume(sent)
        return sent


class CubeTransfers:
    def __init__(self, dp_size, fsdp_size):
        self.dp_size, self.fsdp_size = dp_size, fsdp_size
        self.slots = [4, 4, 4, 2, 2, 16]
        self.arrived, self.before_core = [], []

    def permute(self, v, axis, size, flip):
        self.arrived.append(lax.ppermute(v, axis, along(axis, size, flip)))
        return self.arrived[-1]

    def take_arrived(self):
        arrived, self.arrived = self.arrived, []
        return arrived

    def core(self, v):
        return self.permute(v, "dp", self.dp_size, 1)

    def x(self, v):
        return self.permute(v, "dp", self.dp_size, 2)

    def y(self, v):
        return self.permute(v, "fsdp", self.fsdp_size, 1)

    def z(self, v, flip):
        return self.permute(v, "fsdp", self.fsdp_size, 2 * flip)

    def far(self, v):
        size = self.dp_size * self.fsdp_size
        return lax.ppermute(v, ("dp", "fsdp"), along(("dp", "fsdp"), size, 2 * self.fsdp_size + 1))

    def all_reduce(self, v, merge, beside=()):
        v = merge(v, self.core(v))
        v = merge(merge(v, self.x(v)), merge(self.y(v), self.far(v)))
        (v,) = tie([v], beside)
        return merge(merge(v, self.z(v, 1)), merge(self.z(v, 2), self.z(v, 3)))

    def all_reduce_steps(self, v, merge):
        (v,) = yield [v]
        v = merge(v, self.core(v))
        (v,) = yield [v]
        v = merge(merge(v, self.x(v)), merge(self.y(v), self.far(v)))
        (v,) = yield [v]
        return merge(merge(v, self.z(v, 1)), merge(self.z(v, 2), self.z(v, 3)))

    def table(self, shard_rows):
        q = lax.axis_index("dp").astype(jnp.int32)
        f = lax.axis_index("fsdp").astype(jnp.int32)
        rows = []
        for core in (0, 1):
            for flip_q, flip_y, slots in ((0, 0, range(4)), (0, 1, range(4)), (2, 0, range(4)), (2, 1, range(4))):
                for j in slots:
                    place = f ^ (2 * j + flip_y)
                    rows.append(place * shard_rows + (q ^ (flip_q + core)) * (shard_rows // self.dp_size))
        return jnp.stack(rows)


    def whole_table(self, shard_rows):
        rows = shard_rows // self.dp_size
        order = [f * shard_rows + q * rows for q in range(self.dp_size) for f in range(self.fsdp_size)]
        return jnp.array(order, jnp.int32)

    def whole_gather(self, gate_in, gate_out, lo, hi, tokens=()):
        place = lax.axis_index("dp").astype(jnp.int32)[None]
        own = pack(place, gate_in, gate_out, lo, hi, gate_in.shape[1] // self.dp_size, tokens)
        return [lax.all_gather(own[0], ("dp", "fsdp"))]


    def begin(self, gate_in, gate_out, lo, hi, tokens=()):
        place = lax.axis_index("dp").astype(jnp.int32)[None]
        own = pack(place, gate_in, gate_out, lo, hi, gate_in.shape[1] // self.dp_size, tokens)
        by_2 = self.z(own, 2)
        by_1 = self.z(jnp.concatenate([own, by_2]), 1)
        return [own, by_1, by_2]

    def spread(self, pieces, tokens=()):
        (held,) = combine([[[(0, 0)], [(1, 0)], [(2, 0)], [(1, 1)]]], pieces, tokens)
        return held, self.y(held), self.x(held)

    def relay(self, arrays, tokens=()):
        held, by_y, by_x = arrays
        half_y, half_x = combine([[[(0, 0)], [(0, 1)]], [[(1, 0)], [(1, 1)]]], [(by_y, 2, 0), (by_x, 2, 1)], tokens)
        return [held, by_y, by_x, self.x(half_y), self.y(half_x)], half_y

    def finish(self, mine):
        return mine + [self.core(v) for v in mine]


    def sums(self, parts):
        held, by_y, by_x, far_x, far_y, other = parts
        (other,) = yield [other]
        other = self.core(other)
        far_x, far_y = yield [low_sum(far_x, other[12:14]), low_sum(far_y, other[14:16])]
        got_x, got_y = self.x(far_x), self.y(far_y)
        by_y = jnp.concatenate([low_sum(by_y[:2], other[4:6], got_x), low_sum(by_y[2:], other[6:8])])
        by_x = jnp.concatenate([low_sum(by_x[:2], other[8:10]), low_sum(by_x[2:], other[10:12], got_y)])
        by_y, by_x = yield [by_y, by_x]
        got_y, got_x = self.y(by_y), self.x(by_x)
        held = [low_sum(*(v[k : k + 1] for v in (held, other, got_y, got_x))) for k in range(4)]
        (sent,) = yield [jnp.concatenate([held[1], held[3]])]
        got = self.z(sent, 1)
        (sent,) = yield [low_sum(held[2], got[1:])]
        own = low_sum(held[0], got[:1], self.z(sent, 2))
        (own,) = yield [own]
        return self.dp_pieces(own)

    def dp_pieces(self, own):
        (by_x,) = tie([self.x(own)], self.before_core)
        return [own, self.core(own), by_x, self.core(by_x)]

    def pieces_table(self, shard_rows):
        q = lax.axis_index("dp").astype(jnp.int32)
        return jnp.stack([(q ^ j) * (shard_rows // self.dp_size) for j in range(4)])


class PlainTransfers:
    def __init__(self, dp_size, fsdp_size):
        self.fsdp_size = fsdp_size
        self.slots = [fsdp_size]

    def all_reduce(self, v, merge, beside=()):
        every = lax.all_gather(v, ("dp", "fsdp"))
        while every.shape[0] > 1:
            half = every.shape[0] // 2
            every = jax.vmap(merge)(every[:half], every[half:])
        return every[0]

    def all_reduce_steps(self, v, merge):
        return self.all_reduce(v, merge)
        yield

    def table(self, shard_rows):
        return jnp.arange(self.fsdp_size, dtype=jnp.int32) * shard_rows

    whole_table = table

    def take_arrived(self):
        return []

    def whole_gather(self, gate_in, gate_out, lo, hi, tokens=()):
        return list(self.spread(self.begin(gate_in, gate_out, lo, hi)))

    def begin(self, gate_in, gate_out, lo, hi, tokens=()):
        return jnp.concatenate([gate_in[lo:hi], gate_out[lo:hi]], axis=-1)

    def spread(self, shard, tokens=()):
        return [lax.all_gather(shard, "fsdp")]

    def relay(self, arrays, tokens=()):
        return arrays, arrays[0]

    def finish(self, mine):
        return mine

    def sums(self, parts):
        own = lax.psum_scatter(parts[0], "fsdp", scatter_dimension=0)
        return [lax.psum(own, "dp")[None]]
        yield

    def pieces_table(self, shard_rows):
        return jnp.zeros((1,), jnp.int32)


def place_kernel(n_pieces, table, *refs):
    pieces = refs[:n_pieces]
    g_in, g_out = refs[-2:]
    pr = pieces[0].shape[2]
    wide = g_in.shape[-1]
    for j, piece in enumerate(pieces):
        row = pl.multiple_of(table[j], pr)
        value = piece[0, 0].astype(F32)
        g_in[0, pl.ds(row, pr), :] = value[:, :wide]
        g_out[0, pl.ds(row, pr), :] = value[:, wide:]


def place_grads(table, pieces, start, shard_rows, previous):
    _, n, pr, width = pieces[0].shape
    wide = 2 * width // 3
    shapes = [
        jax.ShapeDtypeStruct((LAYERS * SECTIONS, shard_rows, wide), F32),
        jax.ShapeDtypeStruct((LAYERS * SECTIONS, shard_rows, width - wide), F32),
    ]
    block = lambda w: pl.BlockSpec((1, shard_rows, w), lambda i, *_: (start + i, 0, 0))
    n_pieces = len(pieces)
    extra = [] if previous is None else list(previous)
    return pl.pallas_call(
        functools.partial(place_kernel, n_pieces),
        grid_spec=pltpu.PrefetchScalarGridSpec(
            num_scalar_prefetch=1,
            grid=(n,),
            in_specs=[pl.BlockSpec((1, 1, pr, width), lambda i, *_: (0, i, 0, 0))] * n_pieces
            + [pl.BlockSpec(memory_space=pl.ANY)] * len(extra),
            out_specs=[block(wide), block(width - wide)],
        ),
        out_shape=shapes,
        input_output_aliases={} if previous is None else {1 + n_pieces: 0, 2 + n_pieces: 1},
        cost_estimate=COST,
        name="place_grads",
    )(table, *pieces, *extra)


def local(
    moves,
    features,
    row_valid,
    micro_batch,
    gains,
    shifts,
    mask_logits,
    thresholds,
    gate_in,
    bias_in,
    gate_out,
    bias_out,
    cotangent,
):
    columns = features.shape[1]
    shard_rows = gate_in.shape[2]
    valid = row_valid.astype(F32)[:, None]
    micro = micro_batch[:, None]
    flat = lambda v: v.reshape((LAYERS * SECTIONS,) + v.shape[2:])
    gate_in, gate_out, bias_in, bias_out = flat(gate_in), flat(gate_out), flat(bias_in), flat(bias_out)
    masks = columns * flat(jax.vmap(jax.vmap(feature_mask))(mask_logits, thresholds))
    masks, bias_in, bias_out = masks[:, None], bias_in[:, None], bias_out[:, None]
    add = lambda a, b: a + b
    begin = lambda j, tokens=(): moves.begin(gate_in, gate_out, *GATHERS[j], tokens)

    gathered, records, stored = [], [], []
    current, hidden = features, None
    _, stats = local_stats(current, None, micro, valid)
    begun = [begin(0)]
    spreads = [moves.spread(begun[0], (stats,))]
    begun.append(begin(1, spreads[0][:1]))
    relayed = [moves.relay(spreads[0], begun[1][1:])]
    whole = moves.whole_gather(gate_in, gate_out, *GATHERS[2], relayed[0][1:])
    spreads.append(moves.spread(begun[1], relayed[0][1:]))
    relayed.append(moves.relay(spreads[1]))
    (stats,) = tie([stats], spreads[1][:1])
    stats = moves.all_reduce(stats, merge_stats)
    for k, (lo, hi) in enumerate(GATHERS):
        layer = lo // SECTIONS
        if lo % SECTIONS == 0:
            if k > 0:
                current, stats = local_stats(current, hidden, micro, valid)
                stats = moves.all_reduce(stats, merge_stats)
            normed, x_turned = norm_rows(current, micro, stats, gains[layer], shifts[layer])
            hidden = normed
            records.append((current, stats, normed, x_turned))
        if k < 2:
            arrays = relayed[k][0]
            if k == 1:
                arrays = [*arrays[:3], *tie(arrays[3:], [hidden])] if len(arrays) > 3 else arrays
            arrays, table = moves.finish(arrays), moves.table(shard_rows)
        else:
            arrays, table = whole, moves.whole_table(shard_rows)
        hidden, *saved = forward_chunk(
            table,
            lo,
            hi,
            hidden,
            normed,
            masks,
            bias_in,
            bias_out,
            arrays,
            0,
            relayed[1][1:] if k == 0 else (),
            current if k == 2 else None,
        )
        stored.append((lo, hi, arrays, table, saved))
    mixed_out = hidden

    carried = cotangent.astype(F32) * valid
    pieces_table = moves.pieces_table(shard_rows)

    def backward(k, gh, tokens):
        lo, hi = GROUPS[k]
        current, stats, normed, x_turned = records[lo // SECTIONS]
        ((start_at, _, arrays, table, saved),) = [g for g in stored if g[0] <= lo and hi <= g[1]]
        return backward_chunk(
            jnp.concatenate([table, moves.table(shard_rows)]),
            lo,
            hi,
            gh,
            normed,
            x_turned,
            masks,
            saved,
            arrays,
            lo - start_at,
            moves.slots,
            tokens,
        )

    moves.take_arrived()
    gh, gn_3, vectors_3, out_3 = backward(3, carried, ())
    sums_3 = Sending(moves.sums(out_3))
    sums_3.send(())
    tokens = sums_3.send(())
    moves.take_arrived()
    gh, gn_2, vectors_2, out_2 = backward(2, gh, tokens)
    sums_2 = Sending(moves.sums(out_2))
    tokens = sums_2.send(())
    current, stats, _, _ = records[1]
    total, pooled = pool_grads(current, micro, stats, [gn_3, gn_2, gh], tokens)
    vectors = jnp.concatenate([vectors_2, vectors_3])
    both_1 = moves.all_reduce(jnp.concatenate([pooled, vectors.reshape(-1, columns)]), add, sums_3.ready or ())
    moves.take_arrived()
    tokens = sums_3.send((both_1,)) + sums_2.send((both_1,))
    carried = carry_grads(current, micro, valid, stats, gains[1], total, both_1[: 2 * MB], carried, tokens)
    gh, gn_1, vectors_1, out_1 = backward(1, carried, ())
    sums_1 = Sending(moves.sums(out_1))
    tokens = sums_1.send(moves.take_arrived())
    moves.take_arrived()
    tokens = sums_3.send(tokens)
    tokens = sums_2.send(tokens)
    tokens = sums_1.send(tokens)
    gh, gn_0, vectors_0, out_0 = backward(0, gh, tokens)
    sums_0 = Sending(moves.sums(out_0))
    tokens = sums_0.send(moves.take_arrived())
    tokens = sums_1.send(tokens)
    tokens = sums_3.send(tokens)
    current, stats, _, _ = records[0]
    total, pooled = pool_grads(current, micro, stats, [gn_1, gn_0, gh], tokens)
    vectors = jnp.concatenate([vectors_0, vectors_1])
    both_0 = Sending(moves.all_reduce_steps(jnp.concatenate([pooled, vectors.reshape(-1, columns)]), add))
    tokens = sums_0.send((total,))
    tokens = sums_2.send(tokens)
    tokens = both_0.send(tokens)
    tokens = sums_0.send(tokens)
    tokens = sums_1.send(tokens)
    tokens = sums_2.send(tokens)
    tokens = sums_0.send(tokens)
    tokens = sums_3.send(tokens)
    grads = place_grads(pieces_table, sums_3.result, 9, shard_rows, None)
    tokens = sums_1.send(tokens)
    tokens = both_0.send([*tokens, *grads])
    tokens = sums_2.send(tokens)
    tokens = sums_0.send(tokens)
    tokens = both_0.send(tokens)
    tokens = sums_1.send(tokens)
    grads = place_grads(pieces_table, sums_2.result, 6, shard_rows, grads)
    both_0 = both_0.result
    carried = carry_grads(current, micro, valid, stats, gains[0], total, both_0[: 2 * MB], carried)
    moves.before_core = [carried]
    tokens = sums_0.send([*tokens, *grads])
    grads = place_grads(pieces_table, sums_1.result, 3, shard_rows, grads)
    grads = place_grads(pieces_table, sums_0.result, 0, shard_rows, grads)
    results = [both_0, both_1]
    pooled = jnp.stack([both[: 2 * MB] for both in results])
    stacked = jnp.stack([both[2 * MB :].reshape(SECTIONS, 4 * columns) for both in results])
    _, mask_pull = jax.vjp(jax.vmap(jax.vmap(feature_mask)), mask_logits, thresholds)
    grad_logits, grad_thresholds = mask_pull(stacked[..., :columns])
    unflat = lambda v: v.reshape((LAYERS, SECTIONS) + v.shape[1:])
    return (
        mixed_out,
        carried,
        jnp.sum(pooled[:, MB:], axis=1),
        jnp.sum(pooled[:, :MB], axis=1),
        grad_logits,
        grad_thresholds,
        unflat(grads[0]),
        stacked[..., columns : 3 * columns],
        unflat(grads[1]),
        stacked[..., 3 * columns :],
    )


def solution(mesh):
    rows = P(("dp", "fsdp"), None)
    row = P(("dp", "fsdp"))
    shard = P(None, None, "fsdp", None)
    in_specs = (rows, row, row, P(), P(), P(), P(), shard, P(), shard, P(), rows)
    out_specs = (rows, rows, P(), P(), P(), P(), shard, P(), shard, P())
    dp_size, fsdp_size = mesh.shape["dp"], mesh.shape["fsdp"]
    kind = CubeTransfers if (dp_size, fsdp_size) == (4, 8) else PlainTransfers
    return jax.shard_map(
        functools.partial(local, kind(dp_size, fsdp_size)),
        mesh=mesh,
        in_specs=in_specs,
        out_specs=out_specs,
        check_vma=False,
    )
```

```python
import functools

import jax
import jax.numpy as jnp
from jax import lax
from jax.experimental import pallas as pl
from jax.experimental.pallas import tpu as pltpu
from jax.sharding import PartitionSpec as P

SECTIONS = 6
LAYERS = 2
MB = 4
BF16 = jnp.bfloat16
F32 = jnp.float32
EPSILON = 1e-05
TILE = 256
COST = pl.CostEstimate(flops=1, bytes_accessed=1, transcendentals=0)
LONG = pl.CostEstimate(flops=2 * 10**10, bytes_accessed=1, transcendentals=0)
VMEM_LIMIT = 60 * 1024 * 1024
GATHERS = ((0, 3), (3, 6), (6, 12))
GROUPS = ((0, 3), (3, 6), (6, 9), (9, 12))


def gate(x):
    return 0.5 * jnp.tanh(0.5 * x) + 0.5


def load_weights(table, arrays, wbuf, sems, n, pr, first):
    for part, lo, hi in ((0, 0, 1), (1, 1, n)):
        if lo == hi:
            continue
        at = 0
        for array in arrays:
            for slot in range(array.shape[0]):
                row = pl.multiple_of(table[at], pr)
                pltpu.make_async_copy(
                    array.at[slot, pl.ds(first + lo, hi - lo)],
                    wbuf.at[pl.ds(lo, hi - lo), pl.ds(row, pr)],
                    sems.at[part],
                ).start()
                at += 1


def wait_weights(wbuf, sems, n, part):
    lo, hi = (0, 1) if part == 0 else (1, n)
    whole = wbuf.at[pl.ds(lo, hi - lo)]
    pltpu.make_async_copy(whole, whole, sems.at[part]).wait()


def forward_kernel(n, first, n_arrays, n_tokens, final, pr, tile, table, *refs):
    base, refs = (refs[0], refs[1:]) if final else (None, refs)
    hidden_in, normed, mask, bias_in, bias_out = refs[:5]
    arrays = refs[5 : 5 + n_arrays]
    refs = refs[n_tokens:]
    hidden_out = refs[5 + n_arrays]
    factors = refs[6 + n_arrays : 11 + n_arrays]
    h_turned, rh_turned = refs[11 + n_arrays : 13 + n_arrays]
    wbuf, hid, sems = refs[13 + n_arrays :]
    step = pl.program_id(0)
    rows, cols = hid.shape

    @pl.when(step == 0)
    def _():
        load_weights(table, arrays, wbuf, sems, n, pr, first)
        hid[...] = hidden_in[...]
        wait_weights(wbuf, sems, n, 0)

    if n > 1:
        @pl.when(step == 1)
        def _():
            wait_weights(wbuf, sems, n, 1)

    w = wbuf.at[step]
    mask_row = mask[0]
    b_in = bias_in[0]
    b_out = bias_out[0]

    for t in range(rows // tile):
        at = slice(t * tile, (t + 1) * tile)
        h = hid[at, :]
        x = normed[at, :]
        low_h = h.astype(BF16)
        first_in = jnp.concatenate([(mask_row * x).astype(BF16), low_h], axis=1)
        pre = jnp.dot(first_in, w[:, : 2 * cols], preferred_element_type=F32) + b_in
        update = gate(pre[:, :cols])
        reset = gate(pre[:, cols:])
        low_rh = (reset * h).astype(BF16)
        second_in = jnp.concatenate([low_rh, x.astype(BF16)], axis=1)
        raw = jnp.dot(second_in, w[:, 2 * cols :], preferred_element_type=F32) + b_out
        cand = jnp.tanh(raw)
        keep = 1.0 - update
        apart = cand - h
        hid[at, :] = h + update * apart
        values = (update * (1.0 - cand * cand), apart * update * keep, h * reset * (1.0 - reset), keep, reset)
        for ref, value in zip(factors, values):
            ref[0, at, :] = value.astype(ref.dtype)
        h_turned[0, :, at] = low_h.T
        rh_turned[0, :, at] = low_rh.T

    @pl.when(step == n - 1)
    def _():
        hidden_out[...] = (base[...] + hid[...]).astype(BF16) if final else hid[...]


def forward_chunk(table, lo, hi, hidden, normed, masks, bias_in, bias_out, arrays, first, tokens=(), base=None, tile=TILE):
    n = hi - lo
    bases = () if base is None else (base,)
    rows, cols = hidden.shape
    pr = arrays[0].shape[2]
    depth = 2 * cols
    whole = pl.BlockSpec((rows, cols), lambda i, *_: (0, 0))
    row = lambda width: pl.BlockSpec((1, 1, width), lambda i, *_: (lo + i, 0, 0))
    per = pl.BlockSpec((1, rows, cols), lambda i, *_: (i, 0, 0))
    turned = pl.BlockSpec((1, cols, rows), lambda i, *_: (i, 0, 0))
    saved = [jax.ShapeDtypeStruct((n, rows, cols), t) for t in (F32,) * 5] + [jax.ShapeDtypeStruct((n, cols, rows), BF16)] * 2
    return pl.pallas_call(
        functools.partial(forward_kernel, n, first, len(arrays), len(tokens), base is not None, pr, tile),
        grid_spec=pltpu.PrefetchScalarGridSpec(
            num_scalar_prefetch=1,
            grid=(n,),
            in_specs=[whole] * len(bases) + [whole, whole, row(cols), row(2 * cols), row(cols)]
            + [pl.BlockSpec(memory_space=pl.ANY)] * (len(arrays) + len(tokens)),
            out_specs=[whole] + [per] * 5 + [turned] * 2,
            scratch_shapes=[
                pltpu.VMEM((n, depth, 3 * cols), BF16),
                pltpu.VMEM((rows, cols), F32),
                pltpu.SemaphoreType.DMA((2,)),
            ],
        ),
        out_shape=[jax.ShapeDtypeStruct((rows, cols), F32 if base is None else BF16)] + saved,
        compiler_params=pltpu.CompilerParams(vmem_limit_bytes=VMEM_LIMIT),
        cost_estimate=LONG,
        name="forward_sections",
    )(table, *bases, hidden, normed, masks, bias_in, bias_out, *arrays, *tokens)


def backward_kernel(n, first, n_in, n_out, n_tokens, pr, tile, table, *refs):
    gh_in, normed, x_turned, mask = refs[:4]
    factors = refs[4:9]
    h_turned, rh_turned = refs[9:11]
    arrays = refs[11 : 11 + n_in]
    refs = refs[11 + n_in + n_tokens :]
    gh_out, gn_out, vectors = refs[:3]
    outs = refs[3 : 3 + n_out]
    wbuf, gh, gn, gg, gr, stage, sems, out_sems = refs[3 + n_out :]
    step = pl.program_id(0)
    sec = n - 1 - step
    rows, cols = gh.shape
    wide = 2 * cols

    def wait_out(slot):
        whole = stage.at[slot]
        pltpu.make_async_copy(whole, whole, out_sems.at[slot]).wait()

    @pl.when(step == 0)
    def _():
        for part, lo, hi in ((0, n - 1, n), (1, 0, n - 1)):
            if lo == hi:
                continue
            at = 0
            for array in arrays:
                for slot in range(array.shape[0]):
                    row = pl.multiple_of(table[at], pr)
                    pltpu.make_async_copy(
                        array.at[slot, pl.ds(first + lo, hi - lo)],
                        wbuf.at[pl.ds(lo, hi - lo), pl.ds(row, pr)],
                        sems.at[part],
                    ).start()
                    at += 1
        gh[...] = gh_in[...]
        gn[...] = jnp.zeros_like(gn)
        whole = wbuf.at[pl.ds(n - 1, 1)]
        pltpu.make_async_copy(whole, whole, sems.at[0]).wait()

    if n > 1:
        @pl.when(step == 1)
        def _():
            whole = wbuf.at[pl.ds(0, n - 1)]
            pltpu.make_async_copy(whole, whole, sems.at[1]).wait()

    w = wbuf.at[sec]
    mask_row = mask[0]
    nt = (((1,), (1,)), ((), ()))

    m_sum = jnp.zeros((1, cols), F32)
    bi_sum = jnp.zeros((1, wide), F32)
    bo_sum = jnp.zeros((1, cols), F32)
    for t in range(rows // tile):
        at = slice(t * tile, (t + 1) * tile)
        g = gh[at, :]
        by_raw, by_update, by_reset, keep, reset = (ref[0, at, :].astype(F32) for ref in factors)
        grad_raw = (g * by_raw).astype(BF16)
        gr[at, :] = grad_raw
        second = lax.dot_general(grad_raw, w[:, wide:], nt, preferred_element_type=F32)
        g2 = second[:, :cols]
        gates = jnp.concatenate([(g * by_update).astype(BF16), (g2 * by_reset).astype(BF16)], axis=1)
        gg[at, :] = gates
        first = lax.dot_general(gates, w[:, :wide], nt, preferred_element_type=F32)
        gm = first[:, :cols]
        gn[at, :] = gn[at, :] + second[:, cols:] + gm * mask_row
        gh[at, :] = g * keep + g2 * reset + first[:, cols:]
        m_sum = m_sum + jnp.sum(gm * normed[at, :], axis=0, keepdims=True)
        bi_sum = bi_sum + jnp.sum(gates.astype(F32), axis=0, keepdims=True)
        bo_sum = bo_sum + jnp.sum(grad_raw.astype(F32), axis=0, keepdims=True)
    vectors[0, :, :cols] = m_sum * float(cols)
    vectors[0, :, cols : 3 * cols] = bi_sum
    vectors[0, :, 3 * cols :] = bo_sum

    slot = lax.rem(step, 2)
    if n > 2:
        @pl.when(step >= 2)
        def _():
            wait_out(slot)

    stage[slot, :cols, wide:] = jnp.dot(rh_turned[0], gr[...], preferred_element_type=F32).astype(BF16)
    stage[slot, cols:, wide:] = jnp.dot(x_turned[...], gr[...], preferred_element_type=F32).astype(BF16)
    masked = jnp.dot(x_turned[...], gg[...], preferred_element_type=F32)
    mask_column = jnp.broadcast_to(mask_row, (128, cols)).T[:, :1]
    stage[slot, :cols, :wide] = (masked * mask_column).astype(BF16)
    stage[slot, cols:, :wide] = jnp.dot(h_turned[0], gg[...], preferred_element_type=F32).astype(BF16)

    at = sum(array.shape[0] for array in arrays)
    for out in outs:
        for s in range(out.shape[0]):
            row = pl.multiple_of(table[at], pr)
            pltpu.make_async_copy(stage.at[slot, pl.ds(row, pr)], out.at[s, sec], out_sems.at[slot]).start()
            at += 1

    @pl.when(step == n - 1)
    def _():
        gh_out[...] = gh[...]
        gn_out[...] = gn[...]
        if n > 1:
            wait_out(1 - slot)
        wait_out(slot)


def backward_chunk(table, lo, hi, gh, normed, x_turned, masks, saved, arrays, first, out_slots, tokens=(), tile=TILE):
    n = hi - lo
    rows, cols = gh.shape
    pr = arrays[0].shape[2]
    depth = 2 * cols
    whole = pl.BlockSpec((rows, cols), lambda i, *_: (0, 0))
    row = lambda width: pl.BlockSpec((1, 1, width), lambda i, *_: (hi - 1 - i, 0, 0))
    turned = pl.BlockSpec((1, cols, rows), lambda i, *_: (first + n - 1 - i, 0, 0))
    per = pl.BlockSpec((1, rows, cols), lambda i, *_: (first + n - 1 - i, 0, 0))
    any_spec = pl.BlockSpec(memory_space=pl.ANY)
    state = jax.ShapeDtypeStruct((rows, cols), F32)
    results = pl.pallas_call(
        functools.partial(backward_kernel, n, first, len(arrays), len(out_slots), len(tokens), pr, tile),
        grid_spec=pltpu.PrefetchScalarGridSpec(
            num_scalar_prefetch=1,
            grid=(n,),
            in_specs=[whole, whole, pl.BlockSpec((cols, rows), lambda i, *_: (0, 0)), row(cols)]
            + [per] * 5
            + [turned] * 2
            + [any_spec] * (len(arrays) + len(tokens)),
            out_specs=[whole, whole, pl.BlockSpec((1, 1, 2 * depth), lambda i, *_: (n - 1 - i, 0, 0))] + [any_spec] * len(out_slots),
            scratch_shapes=[
                pltpu.VMEM((n, depth, 3 * cols), BF16),
                pltpu.VMEM((rows, cols), F32),
                pltpu.VMEM((rows, cols), F32),
                pltpu.VMEM((rows, depth), BF16),
                pltpu.VMEM((rows, cols), BF16),
                pltpu.VMEM((2, depth, 3 * cols), BF16),
                pltpu.SemaphoreType.DMA((2,)),
                pltpu.SemaphoreType.DMA((2,)),
            ],
        ),
        out_shape=[state, state, jax.ShapeDtypeStruct((n, 1, 2 * depth), F32)]
        + [jax.ShapeDtypeStruct((s, n, pr, 3 * cols), BF16) for s in out_slots],
        compiler_params=pltpu.CompilerParams(vmem_limit_bytes=VMEM_LIMIT),
        cost_estimate=LONG,
        name="backward_sections",
    )(table, gh, normed, x_turned, masks, *saved, *arrays, *tokens)
    return *results[:3], results[3:]


def pick(micro, table):
    out = table[MB - 1 : MB, :]
    for b in range(MB - 2, -1, -1):
        out = jnp.where(micro == b, table[b : b + 1, :], out)
    return out


def stats_kernel(with_hidden, n_tokens, *refs):
    if with_hidden:
        refs = refs[:4] + refs[4 + n_tokens :]
        u_ref, hidden_ref, micro_ref, valid_ref, out_ref, stats_ref = refs
        u = u_ref[...] + hidden_ref[...]
        out_ref[...] = u
    else:
        u_ref, micro_ref, valid_ref, stats_ref = refs
        u = u_ref[...].astype(F32)
    micro = micro_ref[...]
    valid = valid_ref[...]
    width = u.shape[1]
    counts, means = [], []
    for b in range(MB):
        member = jnp.where(micro == b, valid, 0.0)
        count = jnp.sum(member)
        total = jnp.sum(u * member, axis=0, keepdims=True)
        counts.append(jnp.full((1, width), count, F32))
        means.append(total / jnp.maximum(count, 1.0))
    centred = u - pick(micro, jnp.concatenate(means, axis=0))
    squares = centred * centred * valid
    for b in range(MB):
        stats_ref[b : b + 1, :] = counts[b]
        stats_ref[MB + b : MB + b + 1, :] = means[b]
        stats_ref[2 * MB + b : 2 * MB + b + 1, :] = jnp.sum(jnp.where(micro == b, squares, 0.0), axis=0, keepdims=True)


def local_stats(u, hidden, micro, valid, tokens=()):
    rows, cols = u.shape
    stats = jax.ShapeDtypeStruct((3 * MB, cols), F32)
    args = (u, micro, valid) if hidden is None else (u, hidden, micro, valid)
    out = [stats] if hidden is None else [jax.ShapeDtypeStruct((rows, cols), F32), stats]
    res = pl.pallas_call(
        functools.partial(stats_kernel, hidden is not None, len(tokens)),
        in_specs=[pl.BlockSpec(memory_space=pltpu.VMEM)] * len(args) + [pl.BlockSpec(memory_space=pl.ANY)] * len(tokens),
        out_shape=out,
        compiler_params=pltpu.CompilerParams(vmem_limit_bytes=VMEM_LIMIT),
        cost_estimate=COST,
        name="local_stats",
    )(*args, *tokens)
    return (None, res[0]) if hidden is None else res


def merge_stats(a, b):
    na, ma, qa = a[:MB], a[MB : 2 * MB], a[2 * MB :]
    nb, mb, qb = b[:MB], b[MB : 2 * MB], b[2 * MB :]
    n = na + nb
    inverse = 1.0 / jnp.maximum(n, 1.0)
    apart = ma - mb
    return jnp.concatenate([n, (na * ma + nb * mb) * inverse, qa + qb + apart * apart * (na * nb * inverse)], axis=0)


def norm_kernel(u_ref, micro_ref, stats_ref, gain_ref, shift_ref, normed_ref, turned_ref):
    stats = stats_ref[...]
    scale = lax.rsqrt(stats[2 * MB :] / stats[:MB] + EPSILON)
    micro = micro_ref[...]
    standard = (u_ref[...].astype(F32) - pick(micro, stats[MB : 2 * MB])) * pick(micro, scale)
    normed = standard * gain_ref[...] + shift_ref[...]
    normed_ref[...] = normed
    turned_ref[...] = normed.astype(BF16).T


def norm_rows(u, micro, stats, gain, shift):
    rows, cols = u.shape
    return pl.pallas_call(
        norm_kernel,
        out_shape=[jax.ShapeDtypeStruct((rows, cols), F32), jax.ShapeDtypeStruct((cols, rows), BF16)],
        compiler_params=pltpu.CompilerParams(vmem_limit_bytes=VMEM_LIMIT),
        cost_estimate=COST,
        name="norm_rows",
    )(u, micro, stats, gain[None], shift[None])


def pool_kernel(n_parts, u_ref, micro_ref, stats_ref, *refs):
    parts, (total_ref, pooled_ref) = refs[:n_parts], refs[-2:]
    stats = stats_ref[...]
    scale = lax.rsqrt(stats[2 * MB :] / stats[:MB] + EPSILON)
    micro = micro_ref[...]
    standard = (u_ref[...].astype(F32) - pick(micro, stats[MB : 2 * MB])) * pick(micro, scale)
    total = sum(ref[...] for ref in parts)
    total_ref[...] = total
    product = total * standard
    for b in range(MB):
        pooled_ref[b : b + 1, :] = jnp.sum(jnp.where(micro == b, total, 0.0), axis=0, keepdims=True)
        pooled_ref[MB + b : MB + b + 1, :] = jnp.sum(jnp.where(micro == b, product, 0.0), axis=0, keepdims=True)


def in_vmem(arrays, tokens):
    vmem, any_spec = pl.BlockSpec(memory_space=pltpu.VMEM), pl.BlockSpec(memory_space=pl.ANY)
    return [vmem] * len(arrays) + [any_spec] * len(tokens)


def pool_grads(u, micro, stats, parts, tokens=()):
    rows, cols = u.shape
    args = (u, micro, stats, *parts)
    return pl.pallas_call(
        functools.partial(pool_kernel, len(parts)),
        in_specs=in_vmem(args, tokens),
        out_shape=[jax.ShapeDtypeStruct((rows, cols), F32), jax.ShapeDtypeStruct((2 * MB, cols), F32)],
        compiler_params=pltpu.CompilerParams(vmem_limit_bytes=VMEM_LIMIT),
        cost_estimate=LONG,
        name="pool_grads",
    )(*args, *tokens)


def carry_kernel(u_ref, micro_ref, valid_ref, stats_ref, gain_ref, total_ref, pooled_ref, carried_ref, *refs):
    out_ref = refs[-1]
    stats = stats_ref[...]
    gain = gain_ref[...]
    counts = stats[:MB]
    scale = lax.rsqrt(stats[2 * MB :] / counts + EPSILON)
    pooled = pooled_ref[...]
    micro = micro_ref[...]
    row_scale = pick(micro, scale)
    standard = (u_ref[...].astype(F32) - pick(micro, stats[MB : 2 * MB])) * row_scale
    shift_term = pick(micro, gain * pooled[:MB] / counts)
    scale_term = pick(micro, gain * pooled[MB:] / counts)
    out_ref[...] = carried_ref[...] + row_scale * (
        total_ref[...] * gain - valid_ref[...] * (shift_term + standard * scale_term)
    )


def carry_grads(u, micro, valid, stats, gain, total, pooled, carried, tokens=()):
    rows, cols = u.shape
    args = (u, micro, valid, stats, gain[None], total, pooled, carried)
    return pl.pallas_call(
        carry_kernel,
        in_specs=in_vmem(args, tokens),
        out_shape=jax.ShapeDtypeStruct((rows, cols), F32),
        compiler_params=pltpu.CompilerParams(vmem_limit_bytes=VMEM_LIMIT),
        cost_estimate=COST,
        name="carry_grads",
    )(*args, *tokens)


def feature_mask(logits, thresh):
    centred = logits - jnp.max(logits)
    weights = jnp.exp(centred) * jax.nn.softplus(centred + thresh)
    return weights / jnp.sum(weights)


def combine_kernel(plan, n_in, n_tokens, *refs):
    ins, outs = refs[:n_in], refs[n_in + n_tokens :]
    for out, slots in zip(outs, plan):
        for s, terms in enumerate(slots):
            if len(terms) == 1:
                out[s, 0] = ins[terms[0][0]][terms[0][1], 0]
            else:
                out[s, 0] = sum(ins[k][j, 0].astype(F32) for k, j in terms).astype(out.dtype)


def combine(plan, parts, tokens=()):
    parts = [p if isinstance(p, tuple) else (p, p.shape[0], 0) for p in parts]
    out_n = [{p[0].shape[1] for p, used in zip(parts, uses) if used} for uses in uses_of(plan, len(parts))]
    pr, width = parts[0][0].shape[2:]
    n = max(max(v) for v in out_n)
    step = pr

    def block(slots, at, size):
        if size == n:
            return pl.BlockSpec((slots, 1, step, width), lambda i, r: (at, i, r, 0))
        return pl.BlockSpec((slots, 1, step, width), lambda i, r: (at, jnp.minimum(i, size - 1), r, 0))

    return pl.pallas_call(
        functools.partial(combine_kernel, plan, len(parts), len(tokens)),
        grid=(n, pr // step),
        in_specs=[block(slots, at, a.shape[1]) for a, slots, at in parts]
        + [pl.BlockSpec(memory_space=pl.ANY)] * len(tokens),
        out_specs=[block(len(slots), 0, min(v)) for slots, v in zip(plan, out_n)],
        out_shape=[jax.ShapeDtypeStruct((len(slots), min(v), pr, width), BF16) for slots, v in zip(plan, out_n)],
        compiler_params=pltpu.CompilerParams(vmem_limit_bytes=VMEM_LIMIT),
        cost_estimate=LONG,
        name="combine",
    )(*[p[0] for p in parts], *tokens)


def uses_of(plan, n_parts):
    return [[any(k == part for terms in slots for k, _ in terms) for part in range(n_parts)] for slots in plan]


def pack_kernel(place, g_in, g_out, *refs):
    out = refs[-1]
    wide = g_in.shape[-1]
    out[0, 0, :, :wide] = g_in[0]
    out[0, 0, :, wide:] = g_out[0]


def pack(place, gate_in, gate_out, lo, hi, rows, tokens):
    wide, cols = gate_in.shape[-1], gate_out.shape[-1]
    block = lambda w: pl.BlockSpec((1, rows, w), lambda i, place: (lo + i, place[0], 0))
    return pl.pallas_call(
        pack_kernel,
        grid_spec=pltpu.PrefetchScalarGridSpec(
            num_scalar_prefetch=1,
            grid=(hi - lo,),
            in_specs=[block(wide), block(cols)] + [pl.BlockSpec(memory_space=pl.ANY)] * len(tokens),
            out_specs=pl.BlockSpec((1, 1, rows, wide + cols), lambda i, place: (0, i, 0, 0)),
        ),
        out_shape=jax.ShapeDtypeStruct((1, hi - lo, rows, wide + cols), BF16),
        cost_estimate=COST,
        name="pack",
    )(place, gate_in, gate_out, *tokens)


def along(axis, size, flip):
    return [(i, i ^ flip) for i in range(size)]


def tie_kernel(*refs):
    pass


def tie(arrays, tokens):
    if not tokens:
        return list(arrays)
    any_spec = pl.BlockSpec(memory_space=pl.ANY)
    return pl.pallas_call(
        tie_kernel,
        in_specs=[any_spec] * (len(arrays) + len(tokens)),
        out_specs=[any_spec] * len(arrays),
        out_shape=[jax.ShapeDtypeStruct(a.shape, a.dtype) for a in arrays],
        input_output_aliases={i: i for i in range(len(arrays))},
        cost_estimate=COST,
        name="tie",
    )(*arrays, *tokens)


def low_sum(*terms):
    return sum(v.astype(F32) for v in terms).astype(BF16)


class Sending:
    def __init__(self, steps):
        self.steps, self.ready, self.result = steps, None, None
        self.resume(None)

    def resume(self, sent):
        try:
            self.ready = self.steps.send(sent)
        except StopIteration as stop:
            self.ready, self.result = None, stop.value

    def send(self, tokens):
        if self.ready is None:
            return list(tokens)
        sent = tie(self.ready, list(tokens))
        self.resume(sent)
        return sent


class CubeTransfers:
    def __init__(self, dp_size, fsdp_size):
        self.dp_size, self.fsdp_size = dp_size, fsdp_size
        self.slots = [4, 4, 4, 2, 2, 16]
        self.arrived, self.before_core = [], []

    def permute(self, v, axis, size, flip):
        self.arrived.append(lax.ppermute(v, axis, along(axis, size, flip)))
        return self.arrived[-1]

    def take_arrived(self):
        arrived, self.arrived = self.arrived, []
        return arrived

    def core(self, v):
        return self.permute(v, "dp", self.dp_size, 1)

    def x(self, v):
        return self.permute(v, "dp", self.dp_size, 2)

    def y(self, v):
        return self.permute(v, "fsdp", self.fsdp_size, 1)

    def z(self, v, flip):
        return self.permute(v, "fsdp", self.fsdp_size, 2 * flip)

    def far(self, v):
        size = self.dp_size * self.fsdp_size
        return lax.ppermute(v, ("dp", "fsdp"), along(("dp", "fsdp"), size, 2 * self.fsdp_size + 1))

    def all_reduce(self, v, merge, beside=()):
        v = merge(v, self.core(v))
        v = merge(merge(v, self.x(v)), merge(self.y(v), self.far(v)))
        (v,) = tie([v], beside)
        return merge(merge(v, self.z(v, 1)), merge(self.z(v, 2), self.z(v, 3)))

    def all_reduce_steps(self, v, merge):
        (v,) = yield [v]
        v = merge(v, self.core(v))
        (v,) = yield [v]
        v = merge(merge(v, self.x(v)), merge(self.y(v), self.far(v)))
        (v,) = yield [v]
        return merge(merge(v, self.z(v, 1)), merge(self.z(v, 2), self.z(v, 3)))

    def table(self, shard_rows):
        q = lax.axis_index("dp").astype(jnp.int32)
        f = lax.axis_index("fsdp").astype(jnp.int32)
        rows = []
        for core in (0, 1):
            for flip_q, flip_y, slots in ((0, 0, range(4)), (0, 1, range(4)), (2, 0, range(4)), (2, 1, range(4))):
                for j in slots:
                    place = f ^ (2 * j + flip_y)
                    rows.append(place * shard_rows + (q ^ (flip_q + core)) * (shard_rows // self.dp_size))
        return jnp.stack(rows)


    def whole_table(self, shard_rows):
        rows = shard_rows // self.dp_size
        order = [f * shard_rows + q * rows for q in range(self.dp_size) for f in range(self.fsdp_size)]
        return jnp.array(order, jnp.int32)

    def whole_gather(self, gate_in, gate_out, lo, hi, tokens=()):
        place = lax.axis_index("dp").astype(jnp.int32)[None]
        own = pack(place, gate_in, gate_out, lo, hi, gate_in.shape[1] // self.dp_size, tokens)
        return [lax.all_gather(own[0], ("dp", "fsdp"))]


    def begin(self, gate_in, gate_out, lo, hi, tokens=()):
        place = lax.axis_index("dp").astype(jnp.int32)[None]
        own = pack(place, gate_in, gate_out, lo, hi, gate_in.shape[1] // self.dp_size, tokens)
        return [own] + [self.z(own, j) for j in (1, 2, 3)]

    def spread(self, pieces, tokens=()):
        (held,) = combine([[[(k, 0)] for k in range(4)]], pieces, tokens)
        return held, self.y(held), self.x(held)

    def relay(self, arrays, tokens=()):
        held, by_y, by_x = arrays
        half_y, half_x = combine([[[(0, 0)], [(0, 1)]], [[(1, 0)], [(1, 1)]]], [(by_y, 2, 0), (by_x, 2, 1)], tokens)
        return [held, by_y, by_x, self.x(half_y), self.y(half_x)], half_y

    def finish(self, mine):
        return mine + [self.core(v) for v in mine]


    def sums(self, parts):
        held, by_y, by_x, far_x, far_y, other = parts
        (other,) = yield [other]
        other = self.core(other)
        far_x, far_y = yield [low_sum(far_x, other[12:14]), low_sum(far_y, other[14:16])]
        got_x, got_y = self.x(far_x), self.y(far_y)
        by_y = jnp.concatenate([low_sum(by_y[:2], other[4:6], got_x), low_sum(by_y[2:], other[6:8])])
        by_x = jnp.concatenate([low_sum(by_x[:2], other[8:10]), low_sum(by_x[2:], other[10:12], got_y)])
        by_y, by_x = yield [by_y, by_x]
        got_y, got_x = self.y(by_y), self.x(by_x)
        held = [low_sum(*(v[k : k + 1] for v in (held, other, got_y, got_x))) for k in range(4)]
        (sent,) = yield [jnp.concatenate([held[1], held[3]])]
        got = self.z(sent, 1)
        (sent,) = yield [low_sum(held[2], got[1:])]
        own = low_sum(held[0], got[:1], self.z(sent, 2))
        (own,) = yield [own]
        return self.dp_pieces(own)

    def dp_pieces(self, own):
        (by_x,) = tie([self.x(own)], self.before_core)
        return [own, self.core(own), by_x, self.core(by_x)]

    def pieces_table(self, shard_rows):
        q = lax.axis_index("dp").astype(jnp.int32)
        return jnp.stack([(q ^ j) * (shard_rows // self.dp_size) for j in range(4)])


class PlainTransfers:
    def __init__(self, dp_size, fsdp_size):
        self.fsdp_size = fsdp_size
        self.slots = [fsdp_size]

    def all_reduce(self, v, merge, beside=()):
        every = lax.all_gather(v, ("dp", "fsdp"))
        while every.shape[0] > 1:
            half = every.shape[0] // 2
            every = jax.vmap(merge)(every[:half], every[half:])
        return every[0]

    def all_reduce_steps(self, v, merge):
        return self.all_reduce(v, merge)
        yield

    def table(self, shard_rows):
        return jnp.arange(self.fsdp_size, dtype=jnp.int32) * shard_rows

    whole_table = table

    def take_arrived(self):
        return []

    def whole_gather(self, gate_in, gate_out, lo, hi, tokens=()):
        return list(self.spread(self.begin(gate_in, gate_out, lo, hi)))

    def begin(self, gate_in, gate_out, lo, hi, tokens=()):
        return jnp.concatenate([gate_in[lo:hi], gate_out[lo:hi]], axis=-1)

    def spread(self, shard, tokens=()):
        return [lax.all_gather(shard, "fsdp")]

    def relay(self, arrays, tokens=()):
        return arrays, arrays[0]

    def finish(self, mine):
        return mine

    def sums(self, parts):
        own = lax.psum_scatter(parts[0], "fsdp", scatter_dimension=0)
        return [lax.psum(own, "dp")[None]]
        yield

    def pieces_table(self, shard_rows):
        return jnp.zeros((1,), jnp.int32)


def place_kernel(n_pieces, table, *refs):
    pieces = refs[:n_pieces]
    g_in, g_out = refs[-2:]
    pr = pieces[0].shape[2]
    wide = g_in.shape[-1]
    for j, piece in enumerate(pieces):
        row = pl.multiple_of(table[j], pr)
        for section in range(g_in.shape[0]):
            value = piece[0, section].astype(F32)
            g_in[section, pl.ds(row, pr), :] = value[:, :wide]
            g_out[section, pl.ds(row, pr), :] = value[:, wide:]


def place_grads(table, pieces, start, shard_rows, previous):
    _, n, pr, width = pieces[0].shape
    wide = 2 * width // 3
    shapes = [
        jax.ShapeDtypeStruct((LAYERS * SECTIONS, shard_rows, wide), F32),
        jax.ShapeDtypeStruct((LAYERS * SECTIONS, shard_rows, width - wide), F32),
    ]
    block = lambda w: pl.BlockSpec((n, shard_rows, w), lambda i, *_: (start // n, 0, 0))
    n_pieces = len(pieces)
    extra = [] if previous is None else list(previous)
    return pl.pallas_call(
        functools.partial(place_kernel, n_pieces),
        grid_spec=pltpu.PrefetchScalarGridSpec(
            num_scalar_prefetch=1,
            grid=(1,),
            in_specs=[pl.BlockSpec((1, n, pr, width), lambda i, *_: (0, 0, 0, 0))] * n_pieces
            + [pl.BlockSpec(memory_space=pl.ANY)] * len(extra),
            out_specs=[block(wide), block(width - wide)],
        ),
        out_shape=shapes,
        input_output_aliases={} if previous is None else {1 + n_pieces: 0, 2 + n_pieces: 1},
        cost_estimate=COST,
        name="place_grads",
    )(table, *pieces, *extra)


def local(
    moves,
    features,
    row_valid,
    micro_batch,
    gains,
    shifts,
    mask_logits,
    thresholds,
    gate_in,
    bias_in,
    gate_out,
    bias_out,
    cotangent,
):
    columns = features.shape[1]
    shard_rows = gate_in.shape[2]
    valid = row_valid.astype(F32)[:, None]
    micro = micro_batch[:, None]
    flat = lambda v: v.reshape((LAYERS * SECTIONS,) + v.shape[2:])
    gate_in, gate_out, bias_in, bias_out = flat(gate_in), flat(gate_out), flat(bias_in), flat(bias_out)
    masks = columns * flat(jax.vmap(jax.vmap(feature_mask))(mask_logits, thresholds))
    masks, bias_in, bias_out = masks[:, None], bias_in[:, None], bias_out[:, None]
    add = lambda a, b: a + b
    begin = lambda j, tokens=(): moves.begin(gate_in, gate_out, *GATHERS[j], tokens)

    gathered, records, stored = [], [], []
    current, hidden = features, None
    _, stats = local_stats(current, None, micro, valid)
    begun = [begin(0)]
    spreads = [moves.spread(begun[0], (stats,))]
    begun.append(begin(1, spreads[0][:1]))
    relayed = [moves.relay(spreads[0], begun[1][1:])]
    whole = moves.whole_gather(gate_in, gate_out, *GATHERS[2], relayed[0][1:])
    spreads.append(moves.spread(begun[1], relayed[0][1:]))
    relayed.append(moves.relay(spreads[1]))
    (stats,) = tie([stats], spreads[1][:1])
    stats = moves.all_reduce(stats, merge_stats)
    for k, (lo, hi) in enumerate(GATHERS):
        layer = lo // SECTIONS
        if lo % SECTIONS == 0:
            if k > 0:
                current, stats = local_stats(current, hidden, micro, valid)
                stats = moves.all_reduce(stats, merge_stats)
            normed, x_turned = norm_rows(current, micro, stats, gains[layer], shifts[layer])
            hidden = normed
            records.append((current, stats, normed, x_turned))
        if k < 2:
            arrays = relayed[k][0]
            if k == 1:
                arrays = [*arrays[:3], *tie(arrays[3:], [hidden])] if len(arrays) > 3 else arrays
            arrays, table = moves.finish(arrays), moves.table(shard_rows)
        else:
            arrays, table = whole, moves.whole_table(shard_rows)
        hidden, *saved = forward_chunk(
            table,
            lo,
            hi,
            hidden,
            normed,
            masks,
            bias_in,
            bias_out,
            arrays,
            0,
            relayed[1][1:] if k == 0 else (),
            current if k == 2 else None,
        )
        stored.append((lo, hi, arrays, table, saved))
    mixed_out = hidden

    carried = cotangent.astype(F32) * valid
    pieces_table = moves.pieces_table(shard_rows)

    def backward(k, gh, tokens):
        lo, hi = GROUPS[k]
        current, stats, normed, x_turned = records[lo // SECTIONS]
        ((start_at, _, arrays, table, saved),) = [g for g in stored if g[0] <= lo and hi <= g[1]]
        return backward_chunk(
            jnp.concatenate([table, moves.table(shard_rows)]),
            lo,
            hi,
            gh,
            normed,
            x_turned,
            masks,
            saved,
            arrays,
            lo - start_at,
            moves.slots,
            tokens,
        )

    moves.take_arrived()
    gh, gn_3, vectors_3, out_3 = backward(3, carried, ())
    sums_3 = Sending(moves.sums(out_3))
    sums_3.send(())
    tokens = sums_3.send(())
    moves.take_arrived()
    gh, gn_2, vectors_2, out_2 = backward(2, gh, tokens)
    sums_2 = Sending(moves.sums(out_2))
    tokens = sums_2.send(())
    current, stats, _, _ = records[1]
    total, pooled = pool_grads(current, micro, stats, [gn_3, gn_2, gh], tokens)
    both_1 = moves.all_reduce(pooled, add, sums_3.ready or ())
    tokens = sums_3.send((both_1,)) + sums_2.send((both_1,))
    carried = carry_grads(current, micro, valid, stats, gains[1], total, both_1, carried, tokens)
    gh, gn_1, vectors_1, out_1 = backward(1, carried, ())
    sums_1 = Sending(moves.sums(out_1))
    tokens = sums_1.send(moves.take_arrived())
    moves.take_arrived()
    tokens = sums_3.send(tokens)
    tokens = sums_2.send(tokens)
    tokens = sums_1.send(tokens)
    gh, gn_0, vectors_0, out_0 = backward(0, gh, tokens)
    sums_0 = Sending(moves.sums(out_0))
    tokens = sums_0.send(moves.take_arrived())
    tokens = sums_1.send(tokens)
    tokens = sums_3.send(tokens)
    current, stats, _, _ = records[0]
    total, pooled = pool_grads(current, micro, stats, [gn_1, gn_0, gh], tokens)
    vectors = jnp.concatenate([vectors_0, vectors_1, vectors_2, vectors_3])
    both_0 = Sending(moves.all_reduce_steps(jnp.concatenate([pooled, vectors.reshape(-1, columns)]), add))
    tokens = sums_0.send((total,))
    tokens = sums_2.send(tokens)
    tokens = both_0.send(tokens)
    tokens = sums_0.send(tokens)
    tokens = sums_1.send(tokens)
    tokens = sums_2.send(tokens)
    tokens = sums_0.send(tokens)
    tokens = sums_3.send(tokens)
    grads = place_grads(pieces_table, sums_3.result, 9, shard_rows, None)
    tokens = sums_1.send(tokens)
    tokens = both_0.send([*tokens, *grads])
    tokens = sums_2.send(tokens)
    tokens = sums_0.send(tokens)
    tokens = both_0.send(tokens)
    tokens = sums_1.send(tokens)
    grads = place_grads(pieces_table, sums_2.result, 6, shard_rows, grads)
    both_0 = both_0.result
    carried = carry_grads(current, micro, valid, stats, gains[0], total, both_0[: 2 * MB], carried)
    moves.before_core = [carried]
    tokens = sums_0.send([*tokens, *grads])
    grads = place_grads(pieces_table, sums_1.result, 3, shard_rows, grads)
    grads = place_grads(pieces_table, sums_0.result, 0, shard_rows, grads)
    pooled = jnp.stack([both_0[: 2 * MB], both_1])
    stacked = both_0[2 * MB :].reshape(LAYERS, SECTIONS, 4 * columns)
    _, mask_pull = jax.vjp(jax.vmap(jax.vmap(feature_mask)), mask_logits, thresholds)
    grad_logits, grad_thresholds = mask_pull(stacked[..., :columns])
    unflat = lambda v: v.reshape((LAYERS, SECTIONS) + v.shape[1:])
    return (
        mixed_out,
        carried,
        jnp.sum(pooled[:, MB:], axis=1),
        jnp.sum(pooled[:, :MB], axis=1),
        grad_logits,
        grad_thresholds,
        unflat(grads[0]),
        stacked[..., columns : 3 * columns],
        unflat(grads[1]),
        stacked[..., 3 * columns :],
    )


def solution(mesh):
    rows = P(("dp", "fsdp"), None)
    row = P(("dp", "fsdp"))
    shard = P(None, None, "fsdp", None)
    in_specs = (rows, row, row, P(), P(), P(), P(), shard, P(), shard, P(), rows)
    out_specs = (rows, rows, P(), P(), P(), P(), shard, P(), shard, P())
    dp_size, fsdp_size = mesh.shape["dp"], mesh.shape["fsdp"]
    kind = CubeTransfers if (dp_size, fsdp_size) == (4, 8) else PlainTransfers
    return jax.shard_map(
        functools.partial(local, kind(dp_size, fsdp_size)),
        mesh=mesh,
        in_specs=in_specs,
        out_specs=out_specs,
        check_vma=False,
    )
```

```python
import functools

import jax
import jax.numpy as jnp
from jax import lax
from jax.experimental import pallas as pl
from jax.experimental.pallas import tpu as pltpu
from jax.sharding import PartitionSpec as P

SECTIONS = 6
LAYERS = 2
MB = 4
BF16 = jnp.bfloat16
F32 = jnp.float32
EPSILON = 1e-05
TILE = 256
COST = pl.CostEstimate(flops=1, bytes_accessed=1, transcendentals=0)
LONG = pl.CostEstimate(flops=2 * 10**10, bytes_accessed=1, transcendentals=0)
VMEM_LIMIT = 60 * 1024 * 1024
GATHERS = ((0, 3), (3, 6), (6, 12))
GROUPS = ((0, 3), (3, 6), (6, 9), (9, 12))


def gate(x):
    return 0.5 * jnp.tanh(0.5 * x) + 0.5


def load_weights(table, arrays, wbuf, sems, n, pr, first):
    for part, lo, hi in ((0, 0, 1), (1, 1, n)):
        if lo == hi:
            continue
        at = 0
        for array in arrays:
            for slot in range(array.shape[0]):
                row = pl.multiple_of(table[at], pr)
                pltpu.make_async_copy(
                    array.at[slot, pl.ds(first + lo, hi - lo)],
                    wbuf.at[pl.ds(lo, hi - lo), pl.ds(row, pr)],
                    sems.at[part],
                ).start()
                at += 1


def wait_weights(wbuf, sems, n, part):
    lo, hi = (0, 1) if part == 0 else (1, n)
    whole = wbuf.at[pl.ds(lo, hi - lo)]
    pltpu.make_async_copy(whole, whole, sems.at[part]).wait()


def forward_kernel(n, first, n_arrays, n_tokens, final, pr, tile, table, *refs):
    base, refs = (refs[0], refs[1:]) if final else (None, refs)
    hidden_in, normed, mask, bias_in, bias_out = refs[:5]
    arrays = refs[5 : 5 + n_arrays]
    refs = refs[n_tokens:]
    hidden_out = refs[5 + n_arrays]
    factors = refs[6 + n_arrays : 11 + n_arrays]
    h_turned, rh_turned = refs[11 + n_arrays : 13 + n_arrays]
    wbuf, hid, sems = refs[13 + n_arrays :]
    step = pl.program_id(0)
    rows, cols = hid.shape

    @pl.when(step == 0)
    def _():
        load_weights(table, arrays, wbuf, sems, n, pr, first)
        hid[...] = hidden_in[...]
        wait_weights(wbuf, sems, n, 0)

    if n > 1:
        @pl.when(step == 1)
        def _():
            wait_weights(wbuf, sems, n, 1)

    w = wbuf.at[step]
    mask_row = mask[0]
    b_in = bias_in[0]
    b_out = bias_out[0]

    for t in range(rows // tile):
        at = slice(t * tile, (t + 1) * tile)
        h = hid[at, :]
        x = normed[at, :]
        low_h = h.astype(BF16)
        first_in = jnp.concatenate([(mask_row * x).astype(BF16), low_h], axis=1)
        pre = jnp.dot(first_in, w[:, : 2 * cols], preferred_element_type=F32) + b_in
        update = gate(pre[:, :cols])
        reset = gate(pre[:, cols:])
        low_rh = (reset * h).astype(BF16)
        second_in = jnp.concatenate([low_rh, x.astype(BF16)], axis=1)
        raw = jnp.dot(second_in, w[:, 2 * cols :], preferred_element_type=F32) + b_out
        cand = jnp.tanh(raw)
        keep = 1.0 - update
        apart = cand - h
        hid[at, :] = h + update * apart
        values = (update * (1.0 - cand * cand), apart * update * keep, h * reset * (1.0 - reset), keep, reset)
        for ref, value in zip(factors, values):
            ref[0, at, :] = value.astype(ref.dtype)
        h_turned[0, :, at] = low_h.T
        rh_turned[0, :, at] = low_rh.T

    @pl.when(step == n - 1)
    def _():
        hidden_out[...] = (base[...] + hid[...]).astype(BF16) if final else hid[...]


def forward_chunk(table, lo, hi, hidden, normed, masks, bias_in, bias_out, arrays, first, tokens=(), base=None, tile=TILE):
    n = hi - lo
    bases = () if base is None else (base,)
    rows, cols = hidden.shape
    pr = arrays[0].shape[2]
    depth = 2 * cols
    whole = pl.BlockSpec((rows, cols), lambda i, *_: (0, 0))
    row = lambda width: pl.BlockSpec((1, 1, width), lambda i, *_: (lo + i, 0, 0))
    per = pl.BlockSpec((1, rows, cols), lambda i, *_: (i, 0, 0))
    turned = pl.BlockSpec((1, cols, rows), lambda i, *_: (i, 0, 0))
    saved = [jax.ShapeDtypeStruct((n, rows, cols), t) for t in (F32,) * 5] + [jax.ShapeDtypeStruct((n, cols, rows), BF16)] * 2
    return pl.pallas_call(
        functools.partial(forward_kernel, n, first, len(arrays), len(tokens), base is not None, pr, tile),
        grid_spec=pltpu.PrefetchScalarGridSpec(
            num_scalar_prefetch=1,
            grid=(n,),
            in_specs=[whole] * len(bases) + [whole, whole, row(cols), row(2 * cols), row(cols)]
            + [pl.BlockSpec(memory_space=pl.ANY)] * (len(arrays) + len(tokens)),
            out_specs=[whole] + [per] * 5 + [turned] * 2,
            scratch_shapes=[
                pltpu.VMEM((n, depth, 3 * cols), BF16),
                pltpu.VMEM((rows, cols), F32),
                pltpu.SemaphoreType.DMA((2,)),
            ],
        ),
        out_shape=[jax.ShapeDtypeStruct((rows, cols), F32 if base is None else BF16)] + saved,
        compiler_params=pltpu.CompilerParams(vmem_limit_bytes=VMEM_LIMIT),
        cost_estimate=LONG,
        name="forward_sections",
    )(table, *bases, hidden, normed, masks, bias_in, bias_out, *arrays, *tokens)


def backward_kernel(n, first, n_in, n_out, n_tokens, pr, tile, table, *refs):
    gh_in, normed, x_turned, mask = refs[:4]
    factors = refs[4:9]
    h_turned, rh_turned = refs[9:11]
    arrays = refs[11 : 11 + n_in]
    refs = refs[11 + n_in + n_tokens :]
    gh_out, gn_out, vectors = refs[:3]
    outs = refs[3 : 3 + n_out]
    wbuf, gh, gn, gg, gr, stage, sems, out_sems = refs[3 + n_out :]
    step = pl.program_id(0)
    sec = n - 1 - step
    rows, cols = gh.shape
    wide = 2 * cols

    def wait_out(slot):
        whole = stage.at[slot]
        pltpu.make_async_copy(whole, whole, out_sems.at[slot]).wait()

    @pl.when(step == 0)
    def _():
        for part, lo, hi in ((0, n - 1, n), (1, 0, n - 1)):
            if lo == hi:
                continue
            at = 0
            for array in arrays:
                for slot in range(array.shape[0]):
                    row = pl.multiple_of(table[at], pr)
                    pltpu.make_async_copy(
                        array.at[slot, pl.ds(first + lo, hi - lo)],
                        wbuf.at[pl.ds(lo, hi - lo), pl.ds(row, pr)],
                        sems.at[part],
                    ).start()
                    at += 1
        gh[...] = gh_in[...]
        gn[...] = jnp.zeros_like(gn)
        whole = wbuf.at[pl.ds(n - 1, 1)]
        pltpu.make_async_copy(whole, whole, sems.at[0]).wait()

    if n > 1:
        @pl.when(step == 1)
        def _():
            whole = wbuf.at[pl.ds(0, n - 1)]
            pltpu.make_async_copy(whole, whole, sems.at[1]).wait()

    w = wbuf.at[sec]
    mask_row = mask[0]
    nt = (((1,), (1,)), ((), ()))

    m_sum = jnp.zeros((1, cols), F32)
    bi_sum = jnp.zeros((1, wide), F32)
    bo_sum = jnp.zeros((1, cols), F32)
    for t in range(rows // tile):
        at = slice(t * tile, (t + 1) * tile)
        g = gh[at, :]
        by_raw, by_update, by_reset, keep, reset = (ref[0, at, :].astype(F32) for ref in factors)
        grad_raw = (g * by_raw).astype(BF16)
        gr[at, :] = grad_raw
        second = lax.dot_general(grad_raw, w[:, wide:], nt, preferred_element_type=F32)
        g2 = second[:, :cols]
        gates = jnp.concatenate([(g * by_update).astype(BF16), (g2 * by_reset).astype(BF16)], axis=1)
        gg[at, :] = gates
        first = lax.dot_general(gates, w[:, :wide], nt, preferred_element_type=F32)
        gm = first[:, :cols]
        gn[at, :] = gn[at, :] + second[:, cols:] + gm * mask_row
        gh[at, :] = g * keep + g2 * reset + first[:, cols:]
        m_sum = m_sum + jnp.sum(gm * normed[at, :], axis=0, keepdims=True)
        bi_sum = bi_sum + jnp.sum(gates.astype(F32), axis=0, keepdims=True)
        bo_sum = bo_sum + jnp.sum(grad_raw.astype(F32), axis=0, keepdims=True)
    vectors[0, :, :cols] = m_sum * float(cols)
    vectors[0, :, cols : 3 * cols] = bi_sum
    vectors[0, :, 3 * cols :] = bo_sum

    slot = lax.rem(step, 2)
    if n > 2:
        @pl.when(step >= 2)
        def _():
            wait_out(slot)

    stage[slot, :cols, wide:] = jnp.dot(rh_turned[0], gr[...], preferred_element_type=F32).astype(BF16)
    stage[slot, cols:, wide:] = jnp.dot(x_turned[...], gr[...], preferred_element_type=F32).astype(BF16)
    masked = jnp.dot(x_turned[...], gg[...], preferred_element_type=F32)
    mask_column = jnp.broadcast_to(mask_row, (128, cols)).T[:, :1]
    stage[slot, :cols, :wide] = (masked * mask_column).astype(BF16)
    stage[slot, cols:, :wide] = jnp.dot(h_turned[0], gg[...], preferred_element_type=F32).astype(BF16)

    at = sum(array.shape[0] for array in arrays)
    for out in outs:
        for s in range(out.shape[0]):
            row = pl.multiple_of(table[at], pr)
            pltpu.make_async_copy(stage.at[slot, pl.ds(row, pr)], out.at[s, sec], out_sems.at[slot]).start()
            at += 1

    @pl.when(step == n - 1)
    def _():
        gh_out[...] = gh[...]
        gn_out[...] = gn[...]
        if n > 1:
            wait_out(1 - slot)
        wait_out(slot)


def backward_chunk(table, lo, hi, gh, normed, x_turned, masks, saved, arrays, first, out_slots, tokens=(), tile=TILE):
    n = hi - lo
    rows, cols = gh.shape
    pr = arrays[0].shape[2]
    depth = 2 * cols
    whole = pl.BlockSpec((rows, cols), lambda i, *_: (0, 0))
    row = lambda width: pl.BlockSpec((1, 1, width), lambda i, *_: (hi - 1 - i, 0, 0))
    turned = pl.BlockSpec((1, cols, rows), lambda i, *_: (first + n - 1 - i, 0, 0))
    per = pl.BlockSpec((1, rows, cols), lambda i, *_: (first + n - 1 - i, 0, 0))
    any_spec = pl.BlockSpec(memory_space=pl.ANY)
    state = jax.ShapeDtypeStruct((rows, cols), F32)
    results = pl.pallas_call(
        functools.partial(backward_kernel, n, first, len(arrays), len(out_slots), len(tokens), pr, tile),
        grid_spec=pltpu.PrefetchScalarGridSpec(
            num_scalar_prefetch=1,
            grid=(n,),
            in_specs=[whole, whole, pl.BlockSpec((cols, rows), lambda i, *_: (0, 0)), row(cols)]
            + [per] * 5
            + [turned] * 2
            + [any_spec] * (len(arrays) + len(tokens)),
            out_specs=[whole, whole, pl.BlockSpec((1, 1, 2 * depth), lambda i, *_: (n - 1 - i, 0, 0))] + [any_spec] * len(out_slots),
            scratch_shapes=[
                pltpu.VMEM((n, depth, 3 * cols), BF16),
                pltpu.VMEM((rows, cols), F32),
                pltpu.VMEM((rows, cols), F32),
                pltpu.VMEM((rows, depth), BF16),
                pltpu.VMEM((rows, cols), BF16),
                pltpu.VMEM((2, depth, 3 * cols), BF16),
                pltpu.SemaphoreType.DMA((2,)),
                pltpu.SemaphoreType.DMA((2,)),
            ],
        ),
        out_shape=[state, state, jax.ShapeDtypeStruct((n, 1, 2 * depth), F32)]
        + [jax.ShapeDtypeStruct((s, n, pr, 3 * cols), BF16) for s in out_slots],
        compiler_params=pltpu.CompilerParams(vmem_limit_bytes=VMEM_LIMIT),
        cost_estimate=LONG,
        name="backward_sections",
    )(table, gh, normed, x_turned, masks, *saved, *arrays, *tokens)
    return *results[:3], results[3:]


def pick(micro, table):
    out = table[MB - 1 : MB, :]
    for b in range(MB - 2, -1, -1):
        out = jnp.where(micro == b, table[b : b + 1, :], out)
    return out


def stats_kernel(with_hidden, n_tokens, *refs):
    if with_hidden:
        refs = refs[:4] + refs[4 + n_tokens :]
        u_ref, hidden_ref, micro_ref, valid_ref, out_ref, stats_ref = refs
        u = u_ref[...] + hidden_ref[...]
        out_ref[...] = u
    else:
        u_ref, micro_ref, valid_ref, stats_ref = refs
        u = u_ref[...].astype(F32)
    micro = micro_ref[...]
    valid = valid_ref[...]
    width = u.shape[1]
    counts, means = [], []
    for b in range(MB):
        member = jnp.where(micro == b, valid, 0.0)
        count = jnp.sum(member)
        total = jnp.sum(u * member, axis=0, keepdims=True)
        counts.append(jnp.full((1, width), count, F32))
        means.append(total / jnp.maximum(count, 1.0))
    centred = u - pick(micro, jnp.concatenate(means, axis=0))
    squares = centred * centred * valid
    for b in range(MB):
        stats_ref[b : b + 1, :] = counts[b]
        stats_ref[MB + b : MB + b + 1, :] = means[b]
        stats_ref[2 * MB + b : 2 * MB + b + 1, :] = jnp.sum(jnp.where(micro == b, squares, 0.0), axis=0, keepdims=True)


def local_stats(u, hidden, micro, valid, tokens=()):
    rows, cols = u.shape
    stats = jax.ShapeDtypeStruct((3 * MB, cols), F32)
    args = (u, micro, valid) if hidden is None else (u, hidden, micro, valid)
    out = [stats] if hidden is None else [jax.ShapeDtypeStruct((rows, cols), F32), stats]
    res = pl.pallas_call(
        functools.partial(stats_kernel, hidden is not None, len(tokens)),
        in_specs=[pl.BlockSpec(memory_space=pltpu.VMEM)] * len(args) + [pl.BlockSpec(memory_space=pl.ANY)] * len(tokens),
        out_shape=out,
        compiler_params=pltpu.CompilerParams(vmem_limit_bytes=VMEM_LIMIT),
        cost_estimate=COST,
        name="local_stats",
    )(*args, *tokens)
    return (None, res[0]) if hidden is None else res


def merge_stats(a, b):
    na, ma, qa = a[:MB], a[MB : 2 * MB], a[2 * MB :]
    nb, mb, qb = b[:MB], b[MB : 2 * MB], b[2 * MB :]
    n = na + nb
    inverse = 1.0 / jnp.maximum(n, 1.0)
    apart = ma - mb
    return jnp.concatenate([n, (na * ma + nb * mb) * inverse, qa + qb + apart * apart * (na * nb * inverse)], axis=0)


def norm_kernel(u_ref, micro_ref, stats_ref, gain_ref, shift_ref, normed_ref, turned_ref):
    stats = stats_ref[...]
    scale = lax.rsqrt(stats[2 * MB :] / stats[:MB] + EPSILON)
    micro = micro_ref[...]
    standard = (u_ref[...].astype(F32) - pick(micro, stats[MB : 2 * MB])) * pick(micro, scale)
    normed = standard * gain_ref[...] + shift_ref[...]
    normed_ref[...] = normed
    turned_ref[...] = normed.astype(BF16).T


def norm_rows(u, micro, stats, gain, shift):
    rows, cols = u.shape
    return pl.pallas_call(
        norm_kernel,
        out_shape=[jax.ShapeDtypeStruct((rows, cols), F32), jax.ShapeDtypeStruct((cols, rows), BF16)],
        compiler_params=pltpu.CompilerParams(vmem_limit_bytes=VMEM_LIMIT),
        cost_estimate=COST,
        name="norm_rows",
    )(u, micro, stats, gain[None], shift[None])


def pool_kernel(n_parts, u_ref, micro_ref, stats_ref, *refs):
    parts, (total_ref, pooled_ref) = refs[:n_parts], refs[-2:]
    stats = stats_ref[...]
    scale = lax.rsqrt(stats[2 * MB :] / stats[:MB] + EPSILON)
    micro = micro_ref[...]
    standard = (u_ref[...].astype(F32) - pick(micro, stats[MB : 2 * MB])) * pick(micro, scale)
    total = sum(ref[...] for ref in parts)
    total_ref[...] = total
    product = total * standard
    for b in range(MB):
        pooled_ref[b : b + 1, :] = jnp.sum(jnp.where(micro == b, total, 0.0), axis=0, keepdims=True)
        pooled_ref[MB + b : MB + b + 1, :] = jnp.sum(jnp.where(micro == b, product, 0.0), axis=0, keepdims=True)


def in_vmem(arrays, tokens):
    vmem, any_spec = pl.BlockSpec(memory_space=pltpu.VMEM), pl.BlockSpec(memory_space=pl.ANY)
    return [vmem] * len(arrays) + [any_spec] * len(tokens)


def pool_grads(u, micro, stats, parts, tokens=()):
    rows, cols = u.shape
    args = (u, micro, stats, *parts)
    return pl.pallas_call(
        functools.partial(pool_kernel, len(parts)),
        in_specs=in_vmem(args, tokens),
        out_shape=[jax.ShapeDtypeStruct((rows, cols), F32), jax.ShapeDtypeStruct((2 * MB, cols), F32)],
        compiler_params=pltpu.CompilerParams(vmem_limit_bytes=VMEM_LIMIT),
        cost_estimate=LONG,
        name="pool_grads",
    )(*args, *tokens)


def carry_kernel(u_ref, micro_ref, valid_ref, stats_ref, gain_ref, total_ref, pooled_ref, carried_ref, *refs):
    out_ref = refs[-1]
    stats = stats_ref[...]
    gain = gain_ref[...]
    counts = stats[:MB]
    scale = lax.rsqrt(stats[2 * MB :] / counts + EPSILON)
    pooled = pooled_ref[...]
    micro = micro_ref[...]
    row_scale = pick(micro, scale)
    standard = (u_ref[...].astype(F32) - pick(micro, stats[MB : 2 * MB])) * row_scale
    shift_term = pick(micro, gain * pooled[:MB] / counts)
    scale_term = pick(micro, gain * pooled[MB:] / counts)
    out_ref[...] = carried_ref[...] + row_scale * (
        total_ref[...] * gain - valid_ref[...] * (shift_term + standard * scale_term)
    )


def carry_grads(u, micro, valid, stats, gain, total, pooled, carried, tokens=()):
    rows, cols = u.shape
    args = (u, micro, valid, stats, gain[None], total, pooled, carried)
    return pl.pallas_call(
        carry_kernel,
        in_specs=in_vmem(args, tokens),
        out_shape=jax.ShapeDtypeStruct((rows, cols), F32),
        compiler_params=pltpu.CompilerParams(vmem_limit_bytes=VMEM_LIMIT),
        cost_estimate=COST,
        name="carry_grads",
    )(*args, *tokens)


def feature_mask(logits, thresh):
    centred = logits - jnp.max(logits)
    weights = jnp.exp(centred) * jax.nn.softplus(centred + thresh)
    return weights / jnp.sum(weights)


def combine_kernel(plan, n_in, n_tokens, *refs):
    ins, outs = refs[:n_in], refs[n_in + n_tokens :]
    for out, slots in zip(outs, plan):
        for s, terms in enumerate(slots):
            if len(terms) == 1:
                out[s, 0] = ins[terms[0][0]][terms[0][1], 0]
            else:
                out[s, 0] = sum(ins[k][j, 0].astype(F32) for k, j in terms).astype(out.dtype)


def combine(plan, parts, tokens=()):
    parts = [p if isinstance(p, tuple) else (p, p.shape[0], 0) for p in parts]
    out_n = [{p[0].shape[1] for p, used in zip(parts, uses) if used} for uses in uses_of(plan, len(parts))]
    pr, width = parts[0][0].shape[2:]
    n = max(max(v) for v in out_n)
    step = pr

    def block(slots, at, size):
        if size == n:
            return pl.BlockSpec((slots, 1, step, width), lambda i, r: (at, i, r, 0))
        return pl.BlockSpec((slots, 1, step, width), lambda i, r: (at, jnp.minimum(i, size - 1), r, 0))

    return pl.pallas_call(
        functools.partial(combine_kernel, plan, len(parts), len(tokens)),
        grid=(n, pr // step),
        in_specs=[block(slots, at, a.shape[1]) for a, slots, at in parts]
        + [pl.BlockSpec(memory_space=pl.ANY)] * len(tokens),
        out_specs=[block(len(slots), 0, min(v)) for slots, v in zip(plan, out_n)],
        out_shape=[jax.ShapeDtypeStruct((len(slots), min(v), pr, width), BF16) for slots, v in zip(plan, out_n)],
        compiler_params=pltpu.CompilerParams(vmem_limit_bytes=VMEM_LIMIT),
        cost_estimate=LONG,
        name="combine",
    )(*[p[0] for p in parts], *tokens)


def uses_of(plan, n_parts):
    return [[any(k == part for terms in slots for k, _ in terms) for part in range(n_parts)] for slots in plan]


def pack_kernel(place, g_in, g_out, *refs):
    out = refs[-1]
    wide = g_in.shape[-1]
    out[0, 0, :, :wide] = g_in[0]
    out[0, 0, :, wide:] = g_out[0]


def pack(place, gate_in, gate_out, lo, hi, rows, tokens):
    wide, cols = gate_in.shape[-1], gate_out.shape[-1]
    block = lambda w: pl.BlockSpec((1, rows, w), lambda i, place: (lo + i, place[0], 0))
    return pl.pallas_call(
        pack_kernel,
        grid_spec=pltpu.PrefetchScalarGridSpec(
            num_scalar_prefetch=1,
            grid=(hi - lo,),
            in_specs=[block(wide), block(cols)] + [pl.BlockSpec(memory_space=pl.ANY)] * len(tokens),
            out_specs=pl.BlockSpec((1, 1, rows, wide + cols), lambda i, place: (0, i, 0, 0)),
        ),
        out_shape=jax.ShapeDtypeStruct((1, hi - lo, rows, wide + cols), BF16),
        cost_estimate=COST,
        name="pack",
    )(place, gate_in, gate_out, *tokens)


def along(axis, size, flip):
    return [(i, i ^ flip) for i in range(size)]


def tie_kernel(*refs):
    pass


def tie(arrays, tokens):
    if not tokens:
        return list(arrays)
    any_spec = pl.BlockSpec(memory_space=pl.ANY)
    return pl.pallas_call(
        tie_kernel,
        in_specs=[any_spec] * (len(arrays) + len(tokens)),
        out_specs=[any_spec] * len(arrays),
        out_shape=[jax.ShapeDtypeStruct(a.shape, a.dtype) for a in arrays],
        input_output_aliases={i: i for i in range(len(arrays))},
        cost_estimate=COST,
        name="tie",
    )(*arrays, *tokens)


def low_sum(*terms):
    return sum(v.astype(F32) for v in terms).astype(BF16)


class Sending:
    def __init__(self, steps):
        self.steps, self.ready, self.result = steps, None, None
        self.resume(None)

    def resume(self, sent):
        try:
            self.ready = self.steps.send(sent)
        except StopIteration as stop:
            self.ready, self.result = None, stop.value

    def send(self, tokens):
        if self.ready is None:
            return list(tokens)
        sent = tie(self.ready, list(tokens))
        self.resume(sent)
        return sent


class CubeTransfers:
    def __init__(self, dp_size, fsdp_size):
        self.dp_size, self.fsdp_size = dp_size, fsdp_size
        self.slots = [4, 4, 4, 2, 2, 16]
        self.arrived, self.before_core = [], []

    def permute(self, v, axis, size, flip):
        self.arrived.append(lax.ppermute(v, axis, along(axis, size, flip)))
        return self.arrived[-1]

    def take_arrived(self):
        arrived, self.arrived = self.arrived, []
        return arrived

    def core(self, v):
        return self.permute(v, "dp", self.dp_size, 1)

    def x(self, v):
        return self.permute(v, "dp", self.dp_size, 2)

    def y(self, v):
        return self.permute(v, "fsdp", self.fsdp_size, 1)

    def z(self, v, flip):
        return self.permute(v, "fsdp", self.fsdp_size, 2 * flip)

    def far(self, v):
        size = self.dp_size * self.fsdp_size
        return lax.ppermute(v, ("dp", "fsdp"), along(("dp", "fsdp"), size, 2 * self.fsdp_size + 1))

    def all_reduce(self, v, merge, beside=()):
        v = merge(v, self.core(v))
        v = merge(merge(v, self.x(v)), merge(self.y(v), self.far(v)))
        (v,) = tie([v], beside)
        return merge(merge(v, self.z(v, 1)), merge(self.z(v, 2), self.z(v, 3)))

    def all_reduce_steps(self, v, merge):
        (v,) = yield [v]
        v = merge(v, self.core(v))
        (v,) = yield [v]
        v = merge(merge(v, self.x(v)), merge(self.y(v), self.far(v)))
        (v,) = yield [v]
        return merge(merge(v, self.z(v, 1)), merge(self.z(v, 2), self.z(v, 3)))

    def table(self, shard_rows):
        q = lax.axis_index("dp").astype(jnp.int32)
        f = lax.axis_index("fsdp").astype(jnp.int32)
        rows = []
        for core in (0, 1):
            for flip_q, flip_y, slots in ((0, 0, range(4)), (0, 1, range(4)), (2, 0, range(4)), (2, 1, range(4))):
                for j in slots:
                    place = f ^ (2 * j + flip_y)
                    rows.append(place * shard_rows + (q ^ (flip_q + core)) * (shard_rows // self.dp_size))
        return jnp.stack(rows)


    def whole_table(self, shard_rows):
        rows = shard_rows // self.dp_size
        order = [f * shard_rows + q * rows for q in range(self.dp_size) for f in range(self.fsdp_size)]
        return jnp.array(order, jnp.int32)

    def whole_gather(self, gate_in, gate_out, lo, hi, tokens=()):
        place = lax.axis_index("dp").astype(jnp.int32)[None]
        own = pack(place, gate_in, gate_out, lo, hi, gate_in.shape[1] // self.dp_size, tokens)
        return [lax.all_gather(own[0], ("dp", "fsdp"))]


    def begin(self, gate_in, gate_out, lo, hi, tokens=()):
        place = lax.axis_index("dp").astype(jnp.int32)[None]
        own = pack(place, gate_in, gate_out, lo, hi, gate_in.shape[1] // self.dp_size, tokens)
        return [own] + [self.z(own, j) for j in (1, 2, 3)]

    def spread(self, pieces, tokens=()):
        (held,) = combine([[[(k, 0)] for k in range(4)]], pieces, tokens)
        return held, self.y(held), self.x(held)

    def relay(self, arrays, tokens=()):
        held, by_y, by_x = arrays
        half_y, half_x = combine([[[(0, 0)], [(0, 1)]], [[(1, 0)], [(1, 1)]]], [(by_y, 2, 0), (by_x, 2, 1)], tokens)
        return [held, by_y, by_x, self.x(half_y), self.y(half_x)], half_y

    def finish(self, mine):
        return mine + [self.core(v) for v in mine]


    def sums(self, parts):
        held, by_y, by_x, far_x, far_y, other = parts
        (other,) = yield [other]
        other = self.core(other)
        far_x, far_y = yield [low_sum(far_x, other[12:14]), low_sum(far_y, other[14:16])]
        got_x, got_y = self.x(far_x), self.y(far_y)
        by_y = jnp.concatenate([low_sum(by_y[:2], other[4:6], got_x), low_sum(by_y[2:], other[6:8])])
        by_x = jnp.concatenate([low_sum(by_x[:2], other[8:10]), low_sum(by_x[2:], other[10:12], got_y)])
        by_y, by_x = yield [by_y, by_x]
        got_y, got_x = self.y(by_y), self.x(by_x)
        held = [low_sum(*(v[k : k + 1] for v in (held, other, got_y, got_x))) for k in range(4)]
        (sent,) = yield [jnp.concatenate([held[1], held[3]])]
        got = self.z(sent, 1)
        (sent,) = yield [low_sum(held[2], got[1:])]
        own = low_sum(held[0], got[:1], self.z(sent, 2))
        (own,) = yield [own]
        return self.dp_pieces(own)

    def dp_pieces(self, own):
        (by_x,) = tie([self.x(own)], self.before_core)
        return [own, self.core(own), by_x, self.core(by_x)]

    def pieces_table(self, shard_rows):
        q = lax.axis_index("dp").astype(jnp.int32)
        return jnp.stack([(q ^ j) * (shard_rows // self.dp_size) for j in range(4)])


class PlainTransfers:
    def __init__(self, dp_size, fsdp_size):
        self.fsdp_size = fsdp_size
        self.slots = [fsdp_size]

    def all_reduce(self, v, merge, beside=()):
        every = lax.all_gather(v, ("dp", "fsdp"))
        while every.shape[0] > 1:
            half = every.shape[0] // 2
            every = jax.vmap(merge)(every[:half], every[half:])
        return every[0]

    def all_reduce_steps(self, v, merge):
        return self.all_reduce(v, merge)
        yield

    def table(self, shard_rows):
        return jnp.arange(self.fsdp_size, dtype=jnp.int32) * shard_rows

    whole_table = table

    def take_arrived(self):
        return []

    def whole_gather(self, gate_in, gate_out, lo, hi, tokens=()):
        return list(self.spread(self.begin(gate_in, gate_out, lo, hi)))

    def begin(self, gate_in, gate_out, lo, hi, tokens=()):
        return jnp.concatenate([gate_in[lo:hi], gate_out[lo:hi]], axis=-1)

    def spread(self, shard, tokens=()):
        return [lax.all_gather(shard, "fsdp")]

    def relay(self, arrays, tokens=()):
        return arrays, arrays[0]

    def finish(self, mine):
        return mine

    def sums(self, parts):
        own = lax.psum_scatter(parts[0], "fsdp", scatter_dimension=0)
        return [lax.psum(own, "dp")[None]]
        yield

    def pieces_table(self, shard_rows):
        return jnp.zeros((1,), jnp.int32)


def place_kernel(n_pieces, table, *refs):
    pieces = refs[:n_pieces]
    g_in, g_out = refs[-2:]
    pr = pieces[0].shape[2]
    wide = g_in.shape[-1]
    for j, piece in enumerate(pieces):
        row = pl.multiple_of(table[j], pr)
        for section in range(g_in.shape[0]):
            value = piece[0, section].astype(F32)
            g_in[section, pl.ds(row, pr), :] = value[:, :wide]
            g_out[section, pl.ds(row, pr), :] = value[:, wide:]


def place_grads(table, pieces, start, shard_rows, previous):
    _, n, pr, width = pieces[0].shape
    wide = 2 * width // 3
    shapes = [
        jax.ShapeDtypeStruct((LAYERS * SECTIONS, shard_rows, wide), F32),
        jax.ShapeDtypeStruct((LAYERS * SECTIONS, shard_rows, width - wide), F32),
    ]
    block = lambda w: pl.BlockSpec((n, shard_rows, w), lambda i, *_: (start // n, 0, 0))
    n_pieces = len(pieces)
    extra = [] if previous is None else list(previous)
    return pl.pallas_call(
        functools.partial(place_kernel, n_pieces),
        grid_spec=pltpu.PrefetchScalarGridSpec(
            num_scalar_prefetch=1,
            grid=(1,),
            in_specs=[pl.BlockSpec((1, n, pr, width), lambda i, *_: (0, 0, 0, 0))] * n_pieces
            + [pl.BlockSpec(memory_space=pl.ANY)] * len(extra),
            out_specs=[block(wide), block(width - wide)],
        ),
        out_shape=shapes,
        input_output_aliases={} if previous is None else {1 + n_pieces: 0, 2 + n_pieces: 1},
        cost_estimate=COST,
        name="place_grads",
    )(table, *pieces, *extra)


def local(
    moves,
    features,
    row_valid,
    micro_batch,
    gains,
    shifts,
    mask_logits,
    thresholds,
    gate_in,
    bias_in,
    gate_out,
    bias_out,
    cotangent,
):
    columns = features.shape[1]
    shard_rows = gate_in.shape[2]
    valid = row_valid.astype(F32)[:, None]
    micro = micro_batch[:, None]
    flat = lambda v: v.reshape((LAYERS * SECTIONS,) + v.shape[2:])
    gate_in, gate_out, bias_in, bias_out = flat(gate_in), flat(gate_out), flat(bias_in), flat(bias_out)
    masks = columns * flat(jax.vmap(jax.vmap(feature_mask))(mask_logits, thresholds))
    masks, bias_in, bias_out = masks[:, None], bias_in[:, None], bias_out[:, None]
    add = lambda a, b: a + b
    begin = lambda j, tokens=(): moves.begin(gate_in, gate_out, *GATHERS[j], tokens)

    gathered, records, stored = [], [], []
    current, hidden = features, None
    _, stats = local_stats(current, None, micro, valid)
    begun = [begin(0)]
    spreads = [moves.spread(begun[0], (stats,))]
    begun.append(begin(1, spreads[0][:1]))
    relayed = [moves.relay(spreads[0], begun[1][1:])]
    whole = moves.whole_gather(gate_in, gate_out, *GATHERS[2], relayed[0][1:])
    spreads.append(moves.spread(begun[1], relayed[0][1:]))
    relayed.append(moves.relay(spreads[1]))
    (stats,) = tie([stats], spreads[1][:1])
    stats = moves.all_reduce(stats, merge_stats)
    for k, (lo, hi) in enumerate(GATHERS):
        layer = lo // SECTIONS
        if lo % SECTIONS == 0:
            if k > 0:
                current, stats = local_stats(current, hidden, micro, valid)
                stats = moves.all_reduce(stats, merge_stats)
            normed, x_turned = norm_rows(current, micro, stats, gains[layer], shifts[layer])
            hidden = normed
            records.append((current, stats, normed, x_turned))
        if k < 2:
            arrays = relayed[k][0]
            if k == 1:
                arrays = [*arrays[:3], *tie(arrays[3:], [hidden])] if len(arrays) > 3 else arrays
            arrays, table = moves.finish(arrays), moves.table(shard_rows)
        else:
            arrays, table = whole, moves.whole_table(shard_rows)
        hidden, *saved = forward_chunk(
            table,
            lo,
            hi,
            hidden,
            normed,
            masks,
            bias_in,
            bias_out,
            arrays,
            0,
            relayed[1][1:] if k == 0 else (),
            current if k == 2 else None,
        )
        stored.append((lo, hi, arrays, table, saved))
    mixed_out = hidden

    carried = cotangent.astype(F32) * valid
    pieces_table = moves.pieces_table(shard_rows)

    def backward(k, gh, tokens):
        lo, hi = GROUPS[k]
        current, stats, normed, x_turned = records[lo // SECTIONS]
        ((start_at, _, arrays, table, saved),) = [g for g in stored if g[0] <= lo and hi <= g[1]]
        return backward_chunk(
            jnp.concatenate([table, moves.table(shard_rows)]),
            lo,
            hi,
            gh,
            normed,
            x_turned,
            masks,
            saved,
            arrays,
            lo - start_at,
            moves.slots,
            tokens,
        )

    moves.take_arrived()
    gh, gn_3, vectors_3, out_3 = backward(3, carried, ())
    sums_3 = Sending(moves.sums(out_3))
    sums_3.send(())
    tokens = sums_3.send(())
    moves.take_arrived()
    gh, gn_2, vectors_2, out_2 = backward(2, gh, tokens)
    sums_2 = Sending(moves.sums(out_2))
    tokens = sums_2.send(())
    current, stats, _, _ = records[1]
    total, pooled = pool_grads(current, micro, stats, [gn_3, gn_2, gh], tokens)
    both_1 = moves.all_reduce(pooled, add, sums_3.ready or ())
    tokens = sums_3.send((both_1,)) + sums_2.send((both_1,))
    carried = carry_grads(current, micro, valid, stats, gains[1], total, both_1, carried, tokens)
    gh, gn_1, vectors_1, out_1 = backward(1, carried, ())
    sums_1 = Sending(moves.sums(out_1))
    tokens = sums_1.send(moves.take_arrived())
    moves.take_arrived()
    tokens = sums_3.send(tokens)
    tokens = sums_2.send(tokens)
    tokens = sums_1.send(tokens)
    gh, gn_0, vectors_0, out_0 = backward(0, gh, tokens)
    sums_0 = Sending(moves.sums(out_0))
    tokens = sums_0.send(moves.take_arrived())
    tokens = sums_1.send(tokens)
    tokens = sums_3.send(tokens)
    current, stats, _, _ = records[0]
    total, pooled = pool_grads(current, micro, stats, [gn_1, gn_0, gh], tokens)
    vectors = jnp.concatenate([vectors_0, vectors_1, vectors_2, vectors_3])
    both_0 = Sending(moves.all_reduce_steps(jnp.concatenate([pooled, vectors.reshape(-1, columns)]), add))
    tokens = sums_0.send((total,))
    tokens = sums_2.send(tokens)
    tokens = both_0.send(tokens)
    tokens = sums_0.send(tokens)
    tokens = sums_1.send(tokens)
    tokens = sums_2.send(tokens)
    tokens = sums_0.send(tokens)
    tokens = sums_3.send(tokens)
    grads = place_grads(pieces_table, sums_3.result, 9, shard_rows, None)
    tokens = sums_1.send(tokens)
    tokens = both_0.send([*tokens, *grads])
    tokens = sums_2.send(tokens)
    tokens = sums_0.send(tokens)
    tokens = both_0.send(tokens)
    tokens = sums_1.send(tokens)
    grads = place_grads(pieces_table, sums_2.result, 6, shard_rows, grads)
    both_0 = both_0.result
    carried = carry_grads(current, micro, valid, stats, gains[0], total, both_0[: 2 * MB], carried)
    after = [*tokens, *grads]
    grads = place_grads(pieces_table, sums_1.result, 3, shard_rows, grads)
    moves.before_core = [carried, *grads]
    sums_0.send(after)
    grads = place_grads(pieces_table, sums_0.result, 0, shard_rows, grads)
    pooled = jnp.stack([both_0[: 2 * MB], both_1])
    stacked = both_0[2 * MB :].reshape(LAYERS, SECTIONS, 4 * columns)
    _, mask_pull = jax.vjp(jax.vmap(jax.vmap(feature_mask)), mask_logits, thresholds)
    grad_logits, grad_thresholds = mask_pull(stacked[..., :columns])
    unflat = lambda v: v.reshape((LAYERS, SECTIONS) + v.shape[1:])
    return (
        mixed_out,
        carried,
        jnp.sum(pooled[:, MB:], axis=1),
        jnp.sum(pooled[:, :MB], axis=1),
        grad_logits,
        grad_thresholds,
        unflat(grads[0]),
        stacked[..., columns : 3 * columns],
        unflat(grads[1]),
        stacked[..., 3 * columns :],
    )


def solution(mesh):
    rows = P(("dp", "fsdp"), None)
    row = P(("dp", "fsdp"))
    shard = P(None, None, "fsdp", None)
    in_specs = (rows, row, row, P(), P(), P(), P(), shard, P(), shard, P(), rows)
    out_specs = (rows, rows, P(), P(), P(), P(), shard, P(), shard, P())
    dp_size, fsdp_size = mesh.shape["dp"], mesh.shape["fsdp"]
    kind = CubeTransfers if (dp_size, fsdp_size) == (4, 8) else PlainTransfers
    return jax.shard_map(
        functools.partial(local, kind(dp_size, fsdp_size)),
        mesh=mesh,
        in_specs=in_specs,
        out_specs=out_specs,
        check_vma=False,
    )
```
